128 devices in a mesh: row: 16 (over x, z_lo, core), col: 8 (over y, z_hi).
Axes of the slice: x: 4, y: 4, z: 4 (z_hi: 2, z_lo: 2; z = z_hi * 2 + z_lo), core: 2. Of those that a mesh axis runs over, the one named last changes fastest.
Arguments:
- density: bfloat16 [8192, 8192], P('row', 'col'), may hold values from -0.0625 to 0.0625
- intersection: bfloat16 [8192, 8192], P('row', 'col'), may hold values from -12 to 12
- density_mask: int32 [64, 64], P('row', 'col'), may hold values 0 or 1
- intersection_mask: int32 [64, 64], P('row', 'col'), may hold values 0 or 1
- filter_mask: int32 [64, 64], P('row', 'col'), may hold values 0 or 1
Outputs:
- psp: bfloat16 [8192, 8192], P('row', 'col')
- electrons: float32 [], replicated
The draws below stay inside these ranges and needn't reach their ends.
All inputs are finite; a program needn't handle non-finite values. No bound on the sum of `density_mask` or of `intersection_mask` or of `filter_mask` on one device may be relied on, other than what follows from the above.
Results may differ from the reference program's by a relative error of at most 0.0049.
Values may be sent and summed in bfloat16 or wider, within the bound.
A program may use at most 128 MiB of HBM per device.

```python
import jax
import jax.numpy as jnp

BLOCK = 128
NB = 64
ORDER = 8192


def plant(drawn, stream_key, smallest, high):
    longest = drawn.shape.index(max(drawn.shape))
    spots = []
    for shift in (0, 1):
        where = [jax.random.randint(jax.random.fold_in(stream_key, axis), (), 0, length) for axis, length in enumerate(drawn.shape)]
        where[longest] = (where[longest] + shift) % drawn.shape[longest]
        spots.append(tuple(where))
    return drawn.at[spots[0]].set(smallest).at[spots[1]].set(high)


def level_of(own_key, dims, split, smallest, largest):
    def one(dim, blocks):
        steps = jax.random.uniform(jax.random.fold_in(jax.random.fold_in(own_key, 6), dim), (blocks,), jnp.float32, smallest / len(split), largest / len(split))
        return jnp.repeat(jnp.exp(steps), dims[dim] // blocks).reshape((-1,) + (1,) * (len(dims) - dim - 1))

    loudness = one(*split[0])
    for cut in split[1:]:
        loudness = loudness * one(*cut)
    return loudness


def gaussian(stream_key, dims, spread, most, pieces=(), held_as=jnp.bfloat16):
    drawn = jax.random.normal(stream_key, dims, jnp.float32) * spread
    if len(pieces) > 0:
        drawn = level_of(stream_key, dims, pieces, -0.22, 0.18) * drawn
    return jnp.clip(drawn, min=-most, max=most).astype(held_as)


def setup_inputs(seed: int = 0) -> dict:
    splits = jax.random.split(jax.random.key(seed), 6)
    density = gaussian(splits[0], (ORDER, ORDER), ORDER ** -0.5, 0.0625, ((0, 16), (1, 8)))
    intersection = gaussian(splits[1], (ORDER, ORDER), 2.0, 12.0, ((0, 16), (1, 8)))
    density_mask = plant((jax.random.randint(splits[2], (NB, NB), 0, 2) < 1).astype(jnp.int32), jax.random.fold_in(splits[2], 1), 0, 1)
    intersection_mask = plant((jax.random.randint(splits[3], (NB, NB), 0, 2) < 1).astype(jnp.int32), jax.random.fold_in(splits[3], 1), 0, 1)
    filter_mask = plant((jax.random.randint(splits[4], (NB, NB), 0, 4) < 3).astype(jnp.int32), jax.random.fold_in(splits[4], 1), 0, 1)
    return dict(density=density, intersection=intersection, density_mask=density_mask, intersection_mask=intersection_mask, filter_mask=filter_mask)


def apply_mask(values, mask):
    rows = mask.shape[0]
    cols = mask.shape[1]
    shaped = values.reshape(rows, BLOCK, cols, BLOCK)
    return (shaped * mask.astype(values.dtype)[:, None, :, None]).reshape(values.shape)


def reference(density, intersection, density_mask, intersection_mask, filter_mask):
    left = apply_mask(density, density_mask)
    right = apply_mask(intersection, intersection_mask)
    product = jnp.dot(left, right, preferred_element_type=jnp.float32)
    electrons = jnp.trace(product)
    filtered = apply_mask(product, filter_mask).astype(jnp.bfloat16)
    result = jnp.dot(filtered, left, preferred_element_type=jnp.float32)
    psp = apply_mask(result, filter_mask).astype(jnp.bfloat16)
    return psp, electrons
```

```python
import jax
import jax.numpy as jnp
from jax import lax
from jax.experimental import pallas as pl
from jax.experimental.pallas import tpu as pltpu
from jax.sharding import PartitionSpec as P

BLOCK = 128
ROWS = 512
COLS = 1024
CHUNK = 128
HALF = 256
NTILE = 256
MESH = pl.DeviceIdType.MESH


def kernel(
    dm_ref, im_ref, fm_ref, p_ref, s_ref, o_ref, e_ref,
    pz, a1, s1, b2, fa, acc1, acc2, r1s, r1r, r2s, r2r, eb,
    zs, zr, zfs, zfr, ys, yr, yfs, yfr, ss, sr, sfs, sfr, sds, sdr,
    bs, br, bfs, bfr, bds, bdr, r1ss, r1rs, fs, fr, ffs, ffr, r2ss, r2rs, es, er,
):
    row = lax.axis_index("row")
    col = lax.axis_index("col")
    core = lax.rem(row, 2)
    zl = lax.rem(row // 2, 2)
    x = row // 4
    zh = lax.rem(col, 2)
    y = col // 2
    z = 2 * zh + zl

    def wrap(v):
        return lax.rem(v + 4, 4)

    def dev(x_=x, y_=y, z_=z, c_=core):
        return {"row": x_ * 4 + lax.rem(z_, 2) * 2 + c_, "col": y_ * 2 + z_ // 2}

    xs = [dev(x_=wrap(x + 1)), dev(x_=wrap(x - 1))]
    yd = [dev(y_=wrap(y + 1)), dev(y_=wrap(y - 1))]
    zd = [dev(z_=wrap(z + 1)), dev(z_=wrap(z - 1))]
    x2, y2, z2 = dev(x_=wrap(x + 2)), dev(y_=wrap(y + 2)), dev(z_=wrap(z + 2))
    zp = dev(z_=2 * zh + 1 - zl)
    mate = dev(c_=1 - core)
    xfrom = [wrap(x - 1), wrap(x + 1)]
    zfrom = [wrap(z - 1), wrap(z + 1)]

    peers = xs + yd + zd + [x2, y2, z2, mate]
    barrier = pltpu.get_barrier_semaphore()
    for d in peers:
        pl.semaphore_signal(barrier, inc=1, device_id=d, device_id_type=MESH)
    pl.semaphore_wait(barrier, len(peers))

    sent = []

    def copy(src, dst, ssem, rsem, device):
        return pltpu.make_async_remote_copy(
            src_ref=src, dst_ref=dst, send_sem=ssem, recv_sem=rsem,
            device_id=device, device_id_type=MESH,
        )

    def send(src, dst, ssem, rsem, device):
        cp = copy(src, dst, ssem, rsem, device)
        cp.start()
        sent.append(cp)

    def arrived(ref, ssem, rsem):
        copy(ref, ref, ssem, rsem, mate).wait_recv()

    def rows(j, n=CHUNK):
        return pl.ds(j * n, n)

    def blocks_masked(val, mask_ref, i):
        parts = []
        for b in range(COLS // BLOCK):
            keep = jnp.full((BLOCK, BLOCK), mask_ref[i, b], jnp.int32) != 0
            part = val[:, b * BLOCK:(b + 1) * BLOCK].astype(jnp.float32)
            parts.append(jnp.where(keep, part, 0.0))
        return jnp.concatenate(parts, axis=1).astype(jnp.bfloat16)

    n1, k1 = 1 + zl, 1 - zl
    n2, k2 = 3 * zl, zl

    def send_a(n, k, kk, j):
        src = pz.at[n, rows(j)]
        for d in range(2):
            send(src, a1.at[d, k, rows(j)], ys.at[d, kk, j], yr.at[d, k, j], yd[d])

    own_in_a = zh == zl

    for j in range(4):
        pz[z, rows(j)] = blocks_masked(p_ref[rows(j)], dm_ref, j)
        src = pz.at[z, rows(j)]
        for d in range(2):
            send(src, src, zs.at[d, j], zr.at[d, j], zd[d])
        if j < 2:
            src_y = pz.at[n2, rows(j)]

            @pl.when(own_in_a)
            def _():
                for d in range(2):
                    copy(src_y, a1.at[d, k2, rows(j)], ys.at[d, 1, j], yr.at[d, k2, j], yd[d]).start()

    def s_piece(xx, cc, h):
        return s1.at[xx, pl.ds(pl.multiple_of(cc * ROWS + h * HALF, HALF), HALF)]

    for h in range(2):
        for i in range(2):
            j = 2 * h + i
            s1[x, pl.ds(pl.multiple_of(core * ROWS + j * CHUNK, CHUNK), CHUNK)] = blocks_masked(
                s_ref[rows(j)], im_ref, j)
        src = s_piece(x, core, h)
        for d in range(2):
            send(src, src, ss.at[d, h], sr.at[d, h], xs[d])
        send(src, src, sds.at[0, h], sdr.at[0, h], mate)

    def z_step(j):
        for d in range(2):
            arrived(pz.at[zfrom[d], rows(j)], zs.at[d, j], zr.at[d, j])
        d = j % 2
        src = pz.at[zfrom[d], rows(j)]
        send(src, src, zfs.at[j], zfr.at[j], zd[d])
        send_a(n1, k1, 0, j)

    def z_opp(j):
        arrived(pz.at[wrap(z + 2), rows(j)], zfs.at[j], zfr.at[j])

    def s_step(h):
        for d in range(2):
            src = s_piece(xfrom[d], core, h)
            arrived(src, ss.at[d, h], sr.at[d, h])
            if d == h:
                send(src, src, sfs.at[h], sfr.at[h], xs[d])
            send(src, src, sds.at[1 + d, h], sdr.at[1 + d, h], mate)

    def s_opp(h):
        src = s_piece(wrap(x + 2), core, h)
        arrived(src, sfs.at[h], sfr.at[h])
        send(src, src, sds.at[3, h], sdr.at[3, h], mate)

    def s_mate(i, h):
        xx = [x, xfrom[0], xfrom[1], wrap(x + 2)][i]
        arrived(s_piece(xx, 1 - core, h), sds.at[i, h], sdr.at[i, h])

    z_step(0)
    z_step(1)
    s_step(0)
    for j in (2, 3):
        src = pz.at[n2, rows(j)]

        @pl.when(own_in_a)
        def _():
            for d in range(2):
                copy(src, a1.at[d, k2, rows(j)], ys.at[d, 1, j], yr.at[d, k2, j], yd[d]).start()

    def late_n2(j):
        z_opp(j)
        src = pz.at[n2, rows(j)]
        cps = [copy(src, a1.at[d, k2, rows(j)], ys.at[d, 1, j], yr.at[d, k2, j], yd[d]) for d in range(2)]

        @pl.when(jnp.logical_not(own_in_a))
        def _():
            for cp in cps:
                cp.start()

        sent.extend(cps)

    late_n2(0)
    late_n2(1)
    z_step(2)
    z_step(3)
    s_step(1)
    late_n2(2)
    late_n2(3)

    def b_piece(t, xx, cc, h):
        return b2.at[t, xx, pl.ds(pl.multiple_of(cc * ROWS + h * HALF, HALF), HALF)]

    tile = [2 - zh, 3 * zh]

    def b_start(t):
        for h in range(2):
            src = pz.at[tile[t], rows(h, HALF)]
            for d in range(2):
                send(src, b_piece(t, x, core, h), bs.at[t, d, h], br.at[t, d, h], xs[d])
            send(src, b_piece(t, x, core, h), bds.at[t, 0, h], bdr.at[t, 0, h], mate)
            b2[t, x, pl.ds(pl.multiple_of(core * ROWS + h * HALF, HALF), HALF)] = pz[tile[t], rows(h, HALF)]

    def b_step(t, h):
        for d in range(2):
            src = b_piece(t, xfrom[d], core, h)
            arrived(src, bs.at[t, d, h], br.at[t, d, h])
            if d == h:
                send(src, src, bfs.at[t, h], bfr.at[t, h], xs[d])
            send(src, src, bds.at[t, 1 + d, h], bdr.at[t, 1 + d, h], mate)

    def b_opp(t, h):
        src = b_piece(t, wrap(x + 2), core, h)
        arrived(src, bfs.at[t, h], bfr.at[t, h])
        send(src, src, bds.at[t, 3, h], bdr.at[t, 3, h], mate)

    def b_mate(t, i, h):
        xx = [x, xfrom[0], xfrom[1], wrap(x + 2)][i]
        arrived(b_piece(t, xx, 1 - core, h), bds.at[t, i, h], bdr.at[t, i, h])

    def a_forward(j):
        for d in range(2):
            for k in range(2):
                arrived(a1.at[d, k, rows(j)], ys.at[d, k, j], yr.at[d, k, j])
            src = a1.at[d, d, rows(j)]
            send(src, a1.at[2, d, rows(j)], yfs.at[d, j], yfr.at[d, j], yd[d])

    def a_opp(j):
        for d in range(2):
            arrived(a1.at[2, d, rows(j)], yfs.at[d, j], yfr.at[d, j])

    def ncols(n):
        return pl.ds(pl.multiple_of(n * NTILE, NTILE), NTILE)

    def m1_own(h):
        @pl.loop(0, COLS // NTILE)
        def _(n):
            for k in range(2):
                acc1[k, rows(h, HALF), ncols(n)] = jnp.dot(
                    pz[2 * zl + k, rows(h, HALF)], s1[y, :, ncols(n)], preferred_element_type=jnp.float32)

    def m1(slot, yy, h):
        @pl.loop(0, COLS // NTILE)
        def _(n):
            for k in range(2):
                acc1[k, rows(h, HALF), ncols(n)] += jnp.dot(
                    a1[slot, k, rows(h, HALF)], s1[yy, :, ncols(n)], preferred_element_type=jnp.float32)

    yrel = [wrap(y - 1), wrap(y + 1), wrap(y + 2)]

    def rs1_start(h):
        for j in (2 * h, 2 * h + 1):
            r1s[rows(j)] = acc1[1 - zl, rows(j)].astype(jnp.bfloat16)
            send(r1s.at[rows(j)], r1r.at[rows(j)], r1ss.at[j], r1rs.at[j], zp)

    def f_start(j):
        arrived(r1r.at[rows(j)], r1ss.at[j], r1rs.at[j])
        total = acc1[zl, rows(j)] + r1r[rows(j)].astype(jnp.float32)
        fa[0, rows(j)] = blocks_masked(total, fm_ref, j)
        for d in range(2):
            send(fa.at[0, rows(j)], fa.at[1 + d, rows(j)], fs.at[d, j], fr.at[d, j], yd[d])

    def f_forward(j):
        for d in range(2):
            arrived(fa.at[1 + d, rows(j)], fs.at[d, j], fr.at[d, j])
        d = j % 2
        send(fa.at[1 + d, rows(j)], fa.at[3, rows(j)], ffs.at[j], ffr.at[j], yd[d])

    def f_opp(j):
        arrived(fa.at[3, rows(j)], ffs.at[j], ffr.at[j])

    def diagonal(h):
        at = pl.multiple_of(core * ROWS + h * HALF, HALF)
        square = acc1[zh, rows(h, HALF), pl.ds(at, HALF)]
        r = lax.broadcasted_iota(jnp.int32, (HALF, HALF), 0)
        c = lax.broadcasted_iota(jnp.int32, (HALF, HALF), 1)
        return jnp.sum(jnp.where(r == c, square, 0.0))

    stages = [
        (core, 2, lambda i: dev(c_=lax.rem(core + i, 2))),
        (z, 4, lambda i: dev(z_=lax.rem(z + i, 4))),
        (y, 4, lambda i: dev(y_=lax.rem(y + i, 4))),
        (x, 4, lambda i: dev(x_=lax.rem(x + i, 4))),
    ]

    def e_send(st):
        me, n, target = stages[st]
        for i in range(1, n):
            send(eb.at[st, me], eb.at[st, me], es.at[st, i], er.at[st, i], target(i))

    def e_sum(st):
        me, n, _ = stages[st]
        for i in range(1, n):
            arrived(eb.at[st, lax.rem(me + n - i, n)], es.at[st, i], er.at[st, i])
        total = eb[st, 0]
        for i in range(1, n):
            total = total + eb[st, i]
        return total

    def e_step(st):
        total = e_sum(st)
        eb[st + 1, stages[st + 1][0]] = total
        e_send(st + 1)

    b_start(0)
    s_opp(0)
    s_opp(1)
    b_start(1)
    a_forward(0)
    a_forward(1)
    for i in range(4):
        for h in range(2):
            s_mate(i, h)
    m1_own(0)
    m1(0, yrel[0], 0)
    m1(1, yrel[1], 0)
    a_opp(0)
    a_opp(1)
    m1(2, yrel[2], 0)
    rs1_start(0)
    trace = diagonal(0)
    for h in range(2):
        b_step(0, h)
    m1_own(1)
    a_forward(2)
    a_forward(3)
    f_start(0)
    f_start(1)
    m1(0, yrel[0], 1)
    m1(1, yrel[1], 1)
    for h in range(2):
        b_opp(0, h)
    a_opp(2)
    a_opp(3)
    m1(2, yrel[2], 1)
    rs1_start(1)
    trace = trace + diagonal(1)
    trace = jnp.where(x == y, trace, 0.0)
    eb[0, core] = jnp.full((8, 128), trace, jnp.float32)
    e_send(0)
    f_forward(0)
    f_forward(1)
    f_start(2)
    f_start(3)
    e_step(0)

    def m2(t, slot, yy, start, size, first):
        span = pl.ds(start, size)

        @pl.loop(0, COLS // NTILE)
        def _(n):
            d = jnp.dot(fa[slot, span], b2[t, yy, :, ncols(n)], preferred_element_type=jnp.float32)
            if first:
                acc2[t, span, ncols(n)] = d
            else:
                acc2[t, span, ncols(n)] += d

    def rs2_start(j):
        r2s[rows(j)] = acc2[0, rows(j)].astype(jnp.bfloat16)
        send(r2s.at[rows(j)], r2r.at[rows(j)], r2ss.at[j], r2rs.at[j], z2)

    for i in range(4):
        for h in range(2):
            b_mate(0, i, h)
    f_opp(0)
    f_opp(1)
    m2(0, 0, y, 0, HALF, True)
    for i in range(3):
        m2(0, 1 + i, yrel[i], 0, HALF, False)
    rs2_start(0)
    rs2_start(1)
    e_step(1)
    m2(0, 0, y, HALF, HALF, True)
    for h in range(2):
        b_step(1, h)
    e_step(2)
    f_forward(2)
    f_forward(3)
    for i in range(2):
        m2(0, 1 + i, yrel[i], HALF, HALF, False)
    for h in range(2):
        b_opp(1, h)
    for j in (2, 3):
        f_opp(j)
        m2(0, 3, yrel[2], j * CHUNK, CHUNK, False)
        rs2_start(j)
    for i in range(4):
        for h in range(2):
            b_mate(1, i, h)
    m2(1, 0, y, 0, ROWS, True)
    for i in range(3):
        m2(1, 1 + i, yrel[i], 0, ROWS, False)
    e_ref[...] = e_sum(3)
    for j in range(4):
        arrived(r2r.at[rows(j)], r2ss.at[j], r2rs.at[j])
        total = acc2[1, rows(j)] + r2r[rows(j)].astype(jnp.float32)
        o_ref[rows(j)] = blocks_masked(total, fm_ref, j)
    for cp in sent:
        cp.wait_send()


def shards(density, intersection, density_mask, intersection_mask, filter_mask):
    dma = pltpu.SemaphoreType.DMA
    bf16, f32 = jnp.bfloat16, jnp.float32
    vmem, smem = pl.BlockSpec(memory_space=pltpu.VMEM), pl.BlockSpec(memory_space=pltpu.SMEM)
    psp, electrons = pl.pallas_call(
        kernel,
        out_shape=(jax.ShapeDtypeStruct((ROWS, COLS), bf16), jax.ShapeDtypeStruct((8, 128), f32)),
        in_specs=[smem] * 3 + [vmem] * 2,
        out_specs=(vmem, vmem),
        scratch_shapes=[
            pltpu.VMEM((4, ROWS, COLS), bf16),
            pltpu.VMEM((3, 2, ROWS, COLS), bf16),
            pltpu.VMEM((4, 2 * ROWS, COLS), bf16),
            pltpu.VMEM((2, 4, 2 * ROWS, COLS), bf16),
            pltpu.VMEM((4, ROWS, COLS), bf16),
            pltpu.VMEM((2, ROWS, COLS), f32),
            pltpu.VMEM((2, ROWS, COLS), f32),
            pltpu.VMEM((ROWS, COLS), bf16),
            pltpu.VMEM((ROWS, COLS), bf16),
            pltpu.VMEM((ROWS, COLS), bf16),
            pltpu.VMEM((ROWS, COLS), bf16),
            pltpu.VMEM((4, 4, 8, 128), f32),
            dma((2, 4)), dma((2, 4)), dma((4,)), dma((4,)),
            dma((2, 2, 4)), dma((2, 2, 4)), dma((2, 4)), dma((2, 4)),
            dma((2, 2)), dma((2, 2)), dma((2,)), dma((2,)), dma((4, 2)), dma((4, 2)),
            dma((2, 2, 2)), dma((2, 2, 2)), dma((2, 2)), dma((2, 2)), dma((2, 4, 2)), dma((2, 4, 2)),
            dma((4,)), dma((4,)),
            dma((2, 4)), dma((2, 4)), dma((4,)), dma((4,)),
            dma((4,)), dma((4,)),
            dma((4, 4)), dma((4, 4)),
        ],
        compiler_params=pltpu.CompilerParams(
            collective_id=0, has_side_effects=True, vmem_limit_bytes=62 * 2**20
        ),
        cost_estimate=pl.CostEstimate(flops=17179869184, bytes_accessed=3 * 2**20, transcendentals=0),
    )(density_mask, intersection_mask, filter_mask, density, intersection)
    return psp, electrons[0, 0]


def solution(mesh):
    placed = (P("row", "col"),) * 5
    return jax.shard_map(
        shards, mesh=mesh, in_specs=placed, out_specs=(P("row", "col"), P()), check_vma=False
    )
```

```python
import jax
import jax.numpy as jnp
from jax import lax
from jax.experimental import pallas as pl
from jax.experimental.pallas import tpu as pltpu
from jax.sharding import PartitionSpec as P

BLOCK = 128
ROWS = 512
COLS = 1024
CHUNK = 128
HALF = 256
NTILE = 256
MESH = pl.DeviceIdType.MESH


def kernel(
    dm_ref, im_ref, fm_ref, p_ref, s_ref, o_ref, e_ref,
    pz, yb, yf, a1, s1, b2, fa, acc1, acc2, r1s, r1r, r2s, r2r, eb,
    zs, zr, zfs, zfr, ys, yr, yfs, yfr, ybs, ybr, yzs, yzr, ss, sr, sfs, sfr, sds, sdr,
    bs, br, bfs, bfr, bds, bdr, r1ss, r1rs, fs, fr, ffs, ffr, r2ss, r2rs, es, er,
):
    row = lax.axis_index("row")
    col = lax.axis_index("col")
    core = lax.rem(row, 2)
    zl = lax.rem(row // 2, 2)
    x = row // 4
    zh = lax.rem(col, 2)
    y = col // 2
    z = 2 * zh + zl

    def wrap(v):
        return lax.rem(v + 4, 4)

    def dev(x_=x, y_=y, z_=z, c_=core):
        return {"row": x_ * 4 + lax.rem(z_, 2) * 2 + c_, "col": y_ * 2 + z_ // 2}

    xs = [dev(x_=wrap(x + 1)), dev(x_=wrap(x - 1))]
    yd = [dev(y_=wrap(y + 1)), dev(y_=wrap(y - 1))]
    zd = [dev(z_=wrap(z + 1)), dev(z_=wrap(z - 1))]
    x2, y2, z2 = dev(x_=wrap(x + 2)), dev(y_=wrap(y + 2)), dev(z_=wrap(z + 2))
    zp = dev(z_=2 * zh + 1 - zl)
    mate = dev(c_=1 - core)
    xfrom = [wrap(x - 1), wrap(x + 1)]

    peers = xs + yd + zd + [x2, y2, z2, mate]
    barrier = pltpu.get_barrier_semaphore()
    for d in peers:
        pl.semaphore_signal(barrier, inc=1, device_id=d, device_id_type=MESH)
    pl.semaphore_wait(barrier, len(peers))

    sent = []

    def copy(src, dst, ssem, rsem, device):
        return pltpu.make_async_remote_copy(
            src_ref=src, dst_ref=dst, send_sem=ssem, recv_sem=rsem,
            device_id=device, device_id_type=MESH,
        )

    def send(src, dst, ssem, rsem, device):
        cp = copy(src, dst, ssem, rsem, device)
        cp.start()
        sent.append(cp)

    def arrived(ref, ssem, rsem):
        copy(ref, ref, ssem, rsem, mate).wait_recv()

    def rows(j, n=CHUNK):
        return pl.ds(j * n, n)

    def blocks_masked(val, mask_ref, i):
        parts = []
        for b in range(COLS // BLOCK):
            keep = jnp.full((BLOCK, BLOCK), mask_ref[i, b], jnp.int32) != 0
            part = val[:, b * BLOCK:(b + 1) * BLOCK].astype(jnp.float32)
            parts.append(jnp.where(keep, part, 0.0))
        return jnp.concatenate(parts, axis=1).astype(jnp.bfloat16)

    n1, k1 = 1 + zl, 1 - zl
    n2, k2 = 3 * zl, zl

    def send_a(n, k, kk, j):
        src = pz.at[n, rows(j)]
        for d in range(2):
            send(src, a1.at[d, k, rows(j)], ys.at[d, kk, j], yr.at[d, k, j], yd[d])

    own_in_a = zh == zl
    inside = zh != zl

    nl = jnp.where(own_in_a, 2 - zl, 3 - 3 * zl)

    def zdev(v):
        return dev(z_=v)

    def z_copies(j):
        src = pz.at[z, rows(j)]
        inner = [
            copy(src, src, zs.at[0, j], zr.at[0, j], zdev(3 - z)),
            copy(src, src, zs.at[1, j], zr.at[0, j], zdev(nl)),
        ]
        outer = copy(src, src, zs.at[0, j], zr.at[1, j], zdev(n1))
        return inner, outer

    def z_start(j):
        inner, outer = z_copies(j)

        @pl.when(own_in_a)
        def _():
            outer.start()

        @pl.when(inside)
        def _():
            for cp in inner:
                cp.start()

    def z_step(j):
        arrived(pz.at[n1, rows(j)], zs.at[0, j], zr.at[0, j])
        if j < 2:
            send_a(n1, k1, 0, j)

        @pl.when(inside)
        def _():
            arrived(pz.at[nl, rows(j)], zs.at[0, j], zr.at[1, j])

        src = pz.at[jnp.where(own_in_a, n1, nl), rows(j)]
        send(src, src, zfs.at[j], zfr.at[j], zdev(3 - z))

    def z_far(j):
        @pl.when(inside)
        def _():
            arrived(pz.at[n2, rows(j)], zfs.at[j], zfr.at[j])

    def z_late(j):
        @pl.when(own_in_a)
        def _():
            arrived(pz.at[nl, rows(j)], zfs.at[j], zfr.at[j])

    def z_sent(j):
        inner, outer = z_copies(j)

        @pl.when(own_in_a)
        def _():
            outer.wait_send()

        @pl.when(inside)
        def _():
            for cp in inner:
                cp.wait_send()

    def n2_copies(j):
        src = pz.at[n2, rows(j)]
        return [copy(src, a1.at[d, k2, rows(j)], ys.at[d, 1, j], yr.at[d, k2, j], yd[d]) for d in range(2)]

    def n2_own(j):
        @pl.when(own_in_a)
        def _():
            for cp in n2_copies(j):
                cp.start()

    def n2_far(j):
        @pl.when(inside)
        def _():
            arrived(pz.at[n2, rows(j)], zfs.at[j], zfr.at[j])
            for cp in n2_copies(j):
                cp.start()

        sent.extend(n2_copies(j))

    LAST = 3

    def yb_start():
        for d in range(2):
            send(pz.at[z, rows(LAST)], yb.at[d], ybs.at[d], ybr.at[d], yd[d])

    def yb_step():
        for d in range(2):
            arrived(yb.at[d], ybs.at[d], ybr.at[d])
        for d in range(2):
            part = pl.ds(d * (CHUNK // 2), CHUNK // 2)
            send(yb.at[d, part], yb.at[2, part], yfs.at[d, LAST], yfr.at[d, LAST], yd[d])

    def yb_opp():
        for d in range(2):
            part = pl.ds(d * (CHUNK // 2), CHUNK // 2)
            arrived(yb.at[2, part], yfs.at[d, LAST], yfr.at[d, LAST])

    def yz_copies(i):
        dst = a1.at[i, zl, rows(LAST)]
        near = [
            copy(yb.at[i], dst, yzs.at[0, i], yzr.at[0, i], zdev(3 - z)),
            copy(yb.at[i], dst, yzs.at[1, i], yzr.at[0, i], zdev(nl)),
        ]
        far = copy(yb.at[i], yf.at[i], yzs.at[0, i], yzr.at[1, i], zdev(3 - z))
        return near, far

    def yz_start_outer(i):
        @pl.when(own_in_a)
        def _():
            yz_copies(i)[1].start()
            a1[i, zl, rows(LAST)] = yb[i]

    def yz_start_inner(i):
        @pl.when(inside)
        def _():
            for cp in yz_copies(i)[0]:
                cp.start()

    def yz_pass(i):
        return copy(yf.at[i], a1.at[i, 1 - zl, rows(LAST)], yzs.at[1, i], yzr.at[1, i], zdev(n1))

    def yz_relay(i):
        @pl.when(own_in_a)
        def _():
            arrived(yf.at[i], yzs.at[0, i], yzr.at[1, i])
            yz_pass(i).start()

    def yz_arrived(i):
        arrived(a1.at[i, k1, rows(LAST)], yzs.at[0, i], yzr.at[0, i])

        @pl.when(inside)
        def _():
            arrived(a1.at[i, k2, rows(LAST)], yzs.at[0, i], yzr.at[1, i])

    def yz_sent(i):
        near, far = yz_copies(i)

        @pl.when(own_in_a)
        def _():
            far.wait_send()
            yz_pass(i).wait_send()

        @pl.when(inside)
        def _():
            for cp in near:
                cp.wait_send()

    def p_mask(j):
        pz[z, rows(j)] = blocks_masked(p_ref[rows(j)], dm_ref, j)

    p_mask(LAST)
    yb_start()
    p_mask(0)
    z_start(0)

    def s_piece(xx, cc, h):
        return s1.at[xx, pl.ds(pl.multiple_of(cc * ROWS + h * HALF, HALF), HALF)]

    for h in range(2):
        for i in range(2):
            j = 2 * h + i
            s1[x, pl.ds(pl.multiple_of(core * ROWS + j * CHUNK, CHUNK), CHUNK)] = blocks_masked(
                s_ref[rows(j)], im_ref, j)
        src = s_piece(x, core, h)
        for d in range(2):
            send(src, src, ss.at[d, h], sr.at[d, h], xs[d])
        send(src, src, sds.at[0, h], sdr.at[0, h], mate)

    def s_part(xx, h, d):
        return s1.at[xx, pl.ds(pl.multiple_of(core * ROWS + h * HALF + d * CHUNK, CHUNK), CHUNK)]

    def s_step(h):
        for d in range(2):
            src = s_piece(xfrom[d], core, h)
            arrived(src, ss.at[d, h], sr.at[d, h])
            part = s_part(xfrom[d], h, d)
            send(part, part, sfs.at[d, h], sfr.at[d, h], xs[d])
            send(src, src, sds.at[1 + d, h], sdr.at[1 + d, h], mate)

    def s_opp(h):
        for d in range(2):
            arrived(s_part(wrap(x + 2), h, d), sfs.at[d, h], sfr.at[d, h])
        src = s_piece(wrap(x + 2), core, h)
        send(src, src, sds.at[3, h], sdr.at[3, h], mate)

    def s_mate(i, h):
        xx = [x, xfrom[0], xfrom[1], wrap(x + 2)][i]
        arrived(s_piece(xx, 1 - core, h), sds.at[i, h], sdr.at[i, h])

    tile = [2 - zh, 3 * zh]

    def b_rows(p, xx, cc, off=0, n=HALF):
        return b2.at[p // 2, xx, pl.ds(pl.multiple_of(cc * ROWS + (p % 2) * HALF + off, n), n)]

    def b_start(p):
        src, dst = pz.at[tile[p // 2], rows(p % 2, HALF)], b_rows(p, x, core)
        for d in range(2):
            send(src, dst, bs.at[p, d], br.at[p, d], xs[d])
        send(src, dst, bds.at[p, 0], bdr.at[p, 0], mate)
        dst[...] = src[...]

    def b_step(p):
        for d in range(2):
            src = b_rows(p, xfrom[d], core)
            arrived(src, bs.at[p, d], br.at[p, d])
            part = b_rows(p, xfrom[d], core, d * CHUNK, CHUNK)
            send(part, part, bfs.at[p, d], bfr.at[p, d], xs[d])
            send(src, src, bds.at[p, 1 + d], bdr.at[p, 1 + d], mate)

    def b_opp(p):
        for d in range(2):
            arrived(b_rows(p, wrap(x + 2), core, d * CHUNK, CHUNK), bfs.at[p, d], bfr.at[p, d])
        src = b_rows(p, wrap(x + 2), core)
        send(src, src, bds.at[p, 3], bdr.at[p, 3], mate)

    xrel = [x, xfrom[0], xfrom[1], wrap(x + 2)]

    def b_mate(p, i):
        arrived(b_rows(p, xrel[i], 1 - core), bds.at[p, i], bdr.at[p, i])

    def a_forward(k, kk, j):
        for d in range(2):
            arrived(a1.at[d, k, rows(j)], ys.at[d, kk, j], yr.at[d, k, j])
        src = a1.at[k, k, rows(j)]
        send(src, a1.at[2, k, rows(j)], yfs.at[k, j], yfr.at[k, j], dev(y_=wrap(y + 1 - 2 * k)))

    def a_opp(j):
        for d in range(2):
            arrived(a1.at[2, d, rows(j)], yfs.at[d, j], yfr.at[d, j])

    def ncols(n):
        return pl.ds(pl.multiple_of(n * NTILE, NTILE), NTILE)

    def m1_own(start, size):
        span = pl.ds(start, size)

        @pl.loop(0, COLS // NTILE)
        def _(n):
            for k in range(2):
                acc1[k, span, ncols(n)] = jnp.dot(
                    pz[2 * zl + k, span], s1[y, :, ncols(n)], preferred_element_type=jnp.float32)

    def m1(slot, yy, start, size):
        span = pl.ds(start, size)

        @pl.loop(0, COLS // NTILE)
        def _(n):
            for k in range(2):
                acc1[k, span, ncols(n)] += jnp.dot(
                    a1[slot, k, span], s1[yy, :, ncols(n)], preferred_element_type=jnp.float32)

    yrel = [wrap(y - 1), wrap(y + 1), wrap(y + 2)]

    def rs1_start(j):
        r1s[rows(j)] = acc1[1 - zl, rows(j)].astype(jnp.bfloat16)
        send(r1s.at[rows(j)], r1r.at[rows(j)], r1ss.at[j], r1rs.at[j], zp)

    def f_start(j):
        arrived(r1r.at[rows(j)], r1ss.at[j], r1rs.at[j])
        total = acc1[zl, rows(j)] + r1r[rows(j)].astype(jnp.float32)
        fa[0, rows(j)] = blocks_masked(total, fm_ref, j)
        for d in range(2):
            send(fa.at[0, rows(j)], fa.at[1 + d, rows(j)], fs.at[d, j], fr.at[d, j], yd[d])

    def f_forward(j):
        for d in range(2):
            arrived(fa.at[1 + d, rows(j)], fs.at[d, j], fr.at[d, j])
        d = j % 2
        send(fa.at[1 + d, rows(j)], fa.at[3, rows(j)], ffs.at[j], ffr.at[j], yd[d])

    def f_opp(j):
        arrived(fa.at[3, rows(j)], ffs.at[j], ffr.at[j])

    def diagonal(h):
        at = pl.multiple_of(core * ROWS + h * HALF, HALF)
        square = acc1[zh, rows(h, HALF), pl.ds(at, HALF)]
        r = lax.broadcasted_iota(jnp.int32, (HALF, HALF), 0)
        c = lax.broadcasted_iota(jnp.int32, (HALF, HALF), 1)
        return jnp.sum(jnp.where(r == c, square, 0.0))

    stages = [
        (core, 2, lambda i: dev(c_=lax.rem(core + i, 2))),
        (z, 4, lambda i: dev(z_=lax.rem(z + i, 4))),
        (y, 4, lambda i: dev(y_=lax.rem(y + i, 4))),
        (x, 4, lambda i: dev(x_=lax.rem(x + i, 4))),
    ]

    def e_send(st):
        me, n, target = stages[st]
        for i in range(1, n):
            send(eb.at[st, me], eb.at[st, me], es.at[st, i], er.at[st, i], target(i))

    def e_sum(st):
        me, n, _ = stages[st]
        for i in range(1, n):
            arrived(eb.at[st, lax.rem(me + n - i, n)], es.at[st, i], er.at[st, i])
        total = eb[st, 0]
        for i in range(1, n):
            total = total + eb[st, i]
        return total

    def e_step(st):
        total = e_sum(st)
        eb[st + 1, stages[st + 1][0]] = total
        e_send(st + 1)

    def m2(t, yy, slot, start, size, first):
        span = pl.ds(start, size)

        @pl.loop(0, COLS // NTILE)
        def _(n):
            d = jnp.dot(fa[slot, span], b2[t, yy, :, ncols(n)], preferred_element_type=jnp.float32)
            if first:
                acc2[t, span, ncols(n)] = d
            else:
                acc2[t, span, ncols(n)] += d

    def m2_half(h, xx, first):
        gap = wrap(xx - y)
        slot = jnp.where(gap == 0, 0, jnp.where(gap == 3, 1, jnp.where(gap == 1, 2, 3)))

        @pl.loop(0, COLS // NTILE)
        def _(n):
            d = jnp.zeros((ROWS, NTILE), jnp.float32)
            for c in range(2):
                at = pl.ds(c * ROWS + h * HALF, HALF)
                d += jnp.dot(fa[slot, :, at], b2[1, xx, at, ncols(n)], preferred_element_type=jnp.float32)
            if first:
                acc2[1, :, ncols(n)] = d
            else:
                acc2[1, :, ncols(n)] += d

    def rs2_start(j):
        r2s[rows(j)] = acc2[0, rows(j)].astype(jnp.bfloat16)
        send(r2s.at[rows(j)], r2r.at[rows(j)], r2ss.at[j], r2rs.at[j], z2)

    for j in (1, 2):
        p_mask(j)
    yb_step()
    n2_own(0)
    z_step(0)
    z_start(1)
    yb_opp()
    n2_far(0)
    z_step(1)
    z_start(2)
    n2_own(1)
    a_forward(k1, 0, 0)
    a_forward(k2, 1, 0)
    z_late(0)
    z_late(1)
    b_start(0)
    s_step(0)
    s_step(1)
    for i in range(3):
        yz_start_outer(i)
    n2_far(1)
    z_step(2)
    z_start(3)
    a_forward(k1, 0, 1)
    a_forward(k2, 1, 1)
    send_a(n1, k1, 0, 2)
    n2_own(2)
    z_step(3)
    for i in range(3):
        yz_start_inner(i)
    for i in range(3):
        yz_relay(i)
    n2_far(2)
    s_opp(0)
    s_opp(1)
    b_step(0)
    z_late(2)
    z_late(3)
    b_start(1)
    for i in range(4):
        for h in range(2):
            s_mate(i, h)
    m1_own(0, HALF)
    m1(0, yrel[0], 0, HALF)
    m1(1, yrel[1], 0, HALF)
    a_opp(0)
    a_opp(1)
    m1(2, yrel[2], 0, HALF)
    rs1_start(0)
    rs1_start(1)
    a_forward(k1, 0, 2)
    a_forward(k2, 1, 2)
    b_start(2)
    two, three = 2 * CHUNK, 3 * CHUNK
    m1_own(two, CHUNK)
    m1(0, yrel[0], two, CHUNK)
    m1(1, yrel[1], two, CHUNK)
    f_start(0)
    a_opp(2)
    m1(2, yrel[2], two, CHUNK)
    rs1_start(2)
    f_start(1)
    z_far(3)
    m1_own(three, CHUNK)
    for i in range(3):
        yz_arrived(i)
        m1(i, yrel[i], three, CHUNK)
    rs1_start(3)
    b_step(1)
    f_forward(0)
    f_start(2)
    trace = jnp.where(x == y, diagonal(0) + diagonal(1), 0.0)
    eb[0, core] = jnp.full((8, 128), trace, jnp.float32)
    e_send(0)
    f_forward(1)
    f_start(3)
    b_step(2)
    b_start(3)
    e_step(0)
    b_opp(0)
    b_opp(1)
    for p in range(2):
        for i in range(4):
            b_mate(p, i)
    f_forward(2)
    f_opp(0)
    f_opp(1)
    m2(0, y, 0, 0, HALF, True)
    for i in range(3):
        m2(0, yrel[i], 1 + i, 0, HALF, False)
    rs2_start(0)
    rs2_start(1)
    e_step(1)
    f_forward(3)
    m2(0, y, 0, two, CHUNK, True)
    for i in range(2):
        m2(0, yrel[i], 1 + i, two, CHUNK, False)
    f_opp(2)
    m2(0, yrel[2], 3, two, CHUNK, False)
    rs2_start(2)
    b_opp(2)
    b_step(3)
    m2(0, y, 0, three, CHUNK, True)
    for i in range(2):
        m2(0, yrel[i], 1 + i, three, CHUNK, False)
    e_step(2)
    f_opp(3)
    m2(0, yrel[2], 3, three, CHUNK, False)
    rs2_start(3)
    for h in range(2):
        if h == 1:
            b_opp(3)
        for i in range(4):
            b_mate(2 + h, i)
            m2_half(h, xrel[i], h == 0 and i == 0)
    e_ref[...] = e_sum(3)
    for j in range(4):
        arrived(r2r.at[rows(j)], r2ss.at[j], r2rs.at[j])
        total = acc2[1, rows(j)] + r2r[rows(j)].astype(jnp.float32)
        o_ref[rows(j)] = blocks_masked(total, fm_ref, j)
    for cp in sent:
        cp.wait_send()
    for i in range(3):
        yz_sent(i)
    for j in range(4):
        z_sent(j)


def shards(density, intersection, density_mask, intersection_mask, filter_mask):
    dma = pltpu.SemaphoreType.DMA
    bf16, f32 = jnp.bfloat16, jnp.float32
    vmem, smem = pl.BlockSpec(memory_space=pltpu.VMEM), pl.BlockSpec(memory_space=pltpu.SMEM)
    psp, electrons = pl.pallas_call(
        kernel,
        out_shape=(jax.ShapeDtypeStruct((ROWS, COLS), bf16), jax.ShapeDtypeStruct((8, 128), f32)),
        in_specs=[smem] * 3 + [vmem] * 2,
        out_specs=(vmem, vmem),
        scratch_shapes=[
            pltpu.VMEM((4, ROWS, COLS), bf16),
            pltpu.VMEM((3, CHUNK, COLS), bf16),
            pltpu.VMEM((3, CHUNK, COLS), bf16),
            pltpu.VMEM((3, 2, ROWS, COLS), bf16),
            pltpu.VMEM((4, 2 * ROWS, COLS), bf16),
            pltpu.VMEM((2, 4, 2 * ROWS, COLS), bf16),
            pltpu.VMEM((4, ROWS, COLS), bf16),
            pltpu.VMEM((2, ROWS, COLS), f32),
            pltpu.VMEM((2, ROWS, COLS), f32),
            pltpu.VMEM((ROWS, COLS), bf16),
            pltpu.VMEM((ROWS, COLS), bf16),
            pltpu.VMEM((ROWS, COLS), bf16),
            pltpu.VMEM((ROWS, COLS), bf16),
            pltpu.VMEM((4, 4, 8, 128), f32),
            dma((2, 4)), dma((2, 4)), dma((4,)), dma((4,)),
            dma((2, 2, 4)), dma((2, 2, 4)), dma((2, 4)), dma((2, 4)),
            dma((3,)), dma((3,)), dma((2, 3)), dma((2, 3)),
            dma((2, 2)), dma((2, 2)), dma((2, 2)), dma((2, 2)), dma((4, 2)), dma((4, 2)),
            dma((4, 2)), dma((4, 2)), dma((4, 2)), dma((4, 2)), dma((4, 4)), dma((4, 4)),
            dma((4,)), dma((4,)),
            dma((2, 4)), dma((2, 4)), dma((4,)), dma((4,)),
            dma((4,)), dma((4,)),
            dma((4, 4)), dma((4, 4)),
        ],
        compiler_params=pltpu.CompilerParams(
            collective_id=0, has_side_effects=True, vmem_limit_bytes=62 * 2**20
        ),
        cost_estimate=pl.CostEstimate(flops=17179869184, bytes_accessed=3 * 2**20, transcendentals=0),
    )(density_mask, intersection_mask, filter_mask, density, intersection)
    return psp, electrons[0, 0]


def solution(mesh):
    placed = (P("row", "col"),) * 5
    return jax.shard_map(
        shards, mesh=mesh, in_specs=placed, out_specs=(P("row", "col"), P()), check_vma=False
    )
```

```python
import jax
import jax.numpy as jnp
from jax import lax
from jax.experimental import pallas as pl
from jax.experimental.pallas import tpu as pltpu
from jax.sharding import PartitionSpec as P

BLOCK = 128
ROWS = 512
COLS = 1024
CHUNK = 128
HALF = 256
NTILE = 512
MESH = pl.DeviceIdType.MESH


def kernel(
    dm_ref, im_ref, fm_ref, p_ref, s_ref, o_ref, e_ref,
    pz, yb, yf, a1, s1, b2, fa, acc1, acc2, r1s, r1r, r2s, r2r, eb,
    zs, zr, zfs, zfr, ys, yr, yfs, yfr, ybs, ybr, yzs, yzr, ss, sr, sfs, sfr, sds, sdr,
    bs, br, bfs, bfr, bds, bdr, r1ss, r1rs, fs, fr, ffs, ffr, r2ss, r2rs, es, er,
):
    row = lax.axis_index("row")
    col = lax.axis_index("col")
    core = lax.rem(row, 2)
    zl = lax.rem(row // 2, 2)
    x = row // 4
    zh = lax.rem(col, 2)
    y = col // 2
    z = 2 * zh + zl

    def wrap(v):
        return lax.rem(v + 4, 4)

    def dev(x_=x, y_=y, z_=z, c_=core):
        return {"row": x_ * 4 + lax.rem(z_, 2) * 2 + c_, "col": y_ * 2 + z_ // 2}

    xs = [dev(x_=wrap(x + 1)), dev(x_=wrap(x - 1))]
    yd = [dev(y_=wrap(y + 1)), dev(y_=wrap(y - 1))]
    zd = [dev(z_=wrap(z + 1)), dev(z_=wrap(z - 1))]
    x2, y2, z2 = dev(x_=wrap(x + 2)), dev(y_=wrap(y + 2)), dev(z_=wrap(z + 2))
    zp = dev(z_=2 * zh + 1 - zl)
    mate = dev(c_=1 - core)
    xfrom = [wrap(x - 1), wrap(x + 1)]

    peers = xs + yd + zd + [x2, y2, z2, mate]
    barrier = pltpu.get_barrier_semaphore()
    for d in peers:
        pl.semaphore_signal(barrier, inc=1, device_id=d, device_id_type=MESH)
    pl.semaphore_wait(barrier, len(peers))

    sent = []

    def copy(src, dst, ssem, rsem, device):
        return pltpu.make_async_remote_copy(
            src_ref=src, dst_ref=dst, send_sem=ssem, recv_sem=rsem,
            device_id=device, device_id_type=MESH,
        )

    def send(src, dst, ssem, rsem, device):
        cp = copy(src, dst, ssem, rsem, device)
        cp.start()
        sent.append(cp)

    def arrived(ref, ssem, rsem):
        copy(ref, ref, ssem, rsem, mate).wait_recv()

    def rows(j, n=CHUNK):
        return pl.ds(j * n, n)

    def blocks_masked(val, mask_ref, i):
        parts = []
        for b in range(COLS // BLOCK):
            keep = jnp.full((BLOCK, BLOCK), mask_ref[i, b], jnp.int32) != 0
            part = val[:, b * BLOCK:(b + 1) * BLOCK].astype(jnp.float32)
            parts.append(jnp.where(keep, part, 0.0))
        return jnp.concatenate(parts, axis=1).astype(jnp.bfloat16)

    n1, k1 = 1 + zl, 1 - zl
    n2, k2 = 3 * zl, zl

    def send_a(n, k, kk, j):
        src = pz.at[n, rows(j)]
        for d in range(2):
            send(src, a1.at[d, k, rows(j)], ys.at[d, kk, j], yr.at[d, k, j], yd[d])

    own_in_a = zh == zl
    inside = zh != zl

    nl = jnp.where(own_in_a, 2 - zl, 3 - 3 * zl)

    def zdev(v):
        return dev(z_=v)

    def z_copies(j):
        src = pz.at[z, rows(j)]
        inner = [
            copy(src, src, zs.at[0, j], zr.at[0, j], zdev(3 - z)),
            copy(src, src, zs.at[1, j], zr.at[0, j], zdev(nl)),
        ]
        outer = copy(src, src, zs.at[0, j], zr.at[1, j], zdev(n1))
        return inner, outer

    def z_start(j):
        inner, outer = z_copies(j)

        @pl.when(own_in_a)
        def _():
            outer.start()

        @pl.when(inside)
        def _():
            for cp in inner:
                cp.start()

    def z_step(j):
        arrived(pz.at[n1, rows(j)], zs.at[0, j], zr.at[0, j])
        @pl.when(inside)
        def _():
            arrived(pz.at[nl, rows(j)], zs.at[0, j], zr.at[1, j])

        src = pz.at[jnp.where(own_in_a, n1, nl), rows(j)]
        send(src, src, zfs.at[j], zfr.at[j], zdev(3 - z))

    def z_far(j):
        @pl.when(inside)
        def _():
            arrived(pz.at[n2, rows(j)], zfs.at[j], zfr.at[j])

    def z_late(j):
        @pl.when(own_in_a)
        def _():
            arrived(pz.at[nl, rows(j)], zfs.at[j], zfr.at[j])

    def z_sent(j):
        inner, outer = z_copies(j)

        @pl.when(own_in_a)
        def _():
            outer.wait_send()

        @pl.when(inside)
        def _():
            for cp in inner:
                cp.wait_send()

    def n2_copies(j):
        src = pz.at[n2, rows(j)]
        return [copy(src, a1.at[d, k2, rows(j)], ys.at[d, 1, j], yr.at[d, k2, j], yd[d]) for d in range(2)]

    def n2_own(j):
        @pl.when(own_in_a)
        def _():
            for cp in n2_copies(j):
                cp.start()

    def n2_far(j):
        @pl.when(inside)
        def _():
            arrived(pz.at[n2, rows(j)], zfs.at[j], zfr.at[j])
            for cp in n2_copies(j):
                cp.start()

        sent.extend(n2_copies(j))

    LAST = 3

    def yb_start():
        for d in range(2):
            send(pz.at[z, rows(LAST)], yb.at[d], ybs.at[d], ybr.at[d], yd[d])

    def yb_step():
        for d in range(2):
            arrived(yb.at[d], ybs.at[d], ybr.at[d])
        for d in range(2):
            part = pl.ds(d * (CHUNK // 2), CHUNK // 2)
            send(yb.at[d, part], yb.at[2, part], yfs.at[d, LAST], yfr.at[d, LAST], yd[d])

    def yb_opp():
        for d in range(2):
            part = pl.ds(d * (CHUNK // 2), CHUNK // 2)
            arrived(yb.at[2, part], yfs.at[d, LAST], yfr.at[d, LAST])

    def yz_copies(i):
        dst = a1.at[i, zl, rows(LAST)]
        near = [
            copy(yb.at[i], dst, yzs.at[0, i], yzr.at[0, i], zdev(3 - z)),
            copy(yb.at[i], dst, yzs.at[1, i], yzr.at[0, i], zdev(nl)),
        ]
        far = copy(yb.at[i], yf.at[i], yzs.at[0, i], yzr.at[1, i], zdev(3 - z))
        return near, far

    def yz_start_outer(i):
        @pl.when(own_in_a)
        def _():
            yz_copies(i)[1].start()
            a1[i, zl, rows(LAST)] = yb[i]

    def yz_start_inner(i):
        @pl.when(inside)
        def _():
            for cp in yz_copies(i)[0]:
                cp.start()

    def yz_pass(i):
        return copy(yf.at[i], a1.at[i, 1 - zl, rows(LAST)], yzs.at[1, i], yzr.at[1, i], zdev(n1))

    def yz_relay(i):
        @pl.when(own_in_a)
        def _():
            arrived(yf.at[i], yzs.at[0, i], yzr.at[1, i])
            yz_pass(i).start()

    def yz_arrived(i):
        arrived(a1.at[i, k1, rows(LAST)], yzs.at[0, i], yzr.at[0, i])

        @pl.when(inside)
        def _():
            arrived(a1.at[i, k2, rows(LAST)], yzs.at[0, i], yzr.at[1, i])

    def yz_sent(i):
        near, far = yz_copies(i)

        @pl.when(own_in_a)
        def _():
            far.wait_send()
            yz_pass(i).wait_send()

        @pl.when(inside)
        def _():
            for cp in near:
                cp.wait_send()

    def p_mask(j):
        pz[z, rows(j)] = blocks_masked(p_ref[rows(j)], dm_ref, j)

    p_mask(LAST)
    yb_start()
    p_mask(0)
    z_start(0)

    def s_piece(xx, cc, h):
        return s1.at[xx, pl.ds(pl.multiple_of(cc * ROWS + h * HALF, HALF), HALF)]

    for h in range(2):
        for i in range(2):
            j = 2 * h + i
            s1[x, pl.ds(pl.multiple_of(core * ROWS + j * CHUNK, CHUNK), CHUNK)] = blocks_masked(
                s_ref[rows(j)], im_ref, j)
        src = s_piece(x, core, h)
        for d in range(2):
            send(src, src, ss.at[d, h], sr.at[d, h], xs[d])
        send(src, src, sds.at[0, h], sdr.at[0, h], mate)

    def s_part(xx, h, d):
        return s1.at[xx, pl.ds(pl.multiple_of(core * ROWS + h * HALF + d * CHUNK, CHUNK), CHUNK)]

    def s_step(h):
        for d in range(2):
            src = s_piece(xfrom[d], core, h)
            arrived(src, ss.at[d, h], sr.at[d, h])
            part = s_part(xfrom[d], h, d)
            send(part, part, sfs.at[d, h], sfr.at[d, h], xs[d])
            send(src, src, sds.at[1 + d, h], sdr.at[1 + d, h], mate)

    def s_opp(h):
        for d in range(2):
            arrived(s_part(wrap(x + 2), h, d), sfs.at[d, h], sfr.at[d, h])
        src = s_piece(wrap(x + 2), core, h)
        send(src, src, sds.at[3, h], sdr.at[3, h], mate)

    def s_mate(i, h):
        xx = [x, xfrom[0], xfrom[1], wrap(x + 2)][i]
        arrived(s_piece(xx, 1 - core, h), sds.at[i, h], sdr.at[i, h])

    tile = [2 - zh, 3 * zh]

    def b_rows(p, xx, cc, off=0, n=HALF):
        return b2.at[p // 2, xx, pl.ds(pl.multiple_of(cc * ROWS + (p % 2) * HALF + off, n), n)]

    def b_start(p):
        src, dst = pz.at[tile[p // 2], rows(p % 2, HALF)], b_rows(p, x, core)
        for d in range(2):
            send(src, dst, bs.at[p, d], br.at[p, d], xs[d])
        send(src, dst, bds.at[p, 0], bdr.at[p, 0], mate)
        dst[...] = src[...]

    def b_step(p):
        for d in range(2):
            src = b_rows(p, xfrom[d], core)
            arrived(src, bs.at[p, d], br.at[p, d])
            part = b_rows(p, xfrom[d], core, d * CHUNK, CHUNK)
            send(part, part, bfs.at[p, d], bfr.at[p, d], xs[d])
            send(src, src, bds.at[p, 1 + d], bdr.at[p, 1 + d], mate)

    def b_opp(p):
        for d in range(2):
            arrived(b_rows(p, wrap(x + 2), core, d * CHUNK, CHUNK), bfs.at[p, d], bfr.at[p, d])
        src = b_rows(p, wrap(x + 2), core)
        send(src, src, bds.at[p, 3], bdr.at[p, 3], mate)

    xrel = [x, xfrom[0], xfrom[1], wrap(x + 2)]

    def b_mate(p, i):
        arrived(b_rows(p, xrel[i], 1 - core), bds.at[p, i], bdr.at[p, i])

    def a_forward(k, kk, j):
        for d in range(2):
            arrived(a1.at[d, k, rows(j)], ys.at[d, kk, j], yr.at[d, k, j])
        src = a1.at[k, k, rows(j)]
        send(src, a1.at[2, k, rows(j)], yfs.at[k, j], yfr.at[k, j], dev(y_=wrap(y + 1 - 2 * k)))

    def a_opp(j):
        for d in range(2):
            arrived(a1.at[2, d, rows(j)], yfs.at[d, j], yfr.at[d, j])

    def ncols(n):
        return pl.ds(n * NTILE, NTILE)

    def m1_step(left, yy, start, size, first):
        left = jnp.concatenate(left, axis=0)
        for n in range(COLS // NTILE):
            d = jnp.dot(left, s1[yy, :, ncols(n)], preferred_element_type=jnp.float32)
            for k in range(2):
                span, part = pl.ds(start, size), d[k * size:(k + 1) * size]
                if first:
                    acc1[k, span, ncols(n)] = part
                else:
                    acc1[k, span, ncols(n)] += part

    def m1_own(start, size):
        m1_step([pz[2 * zl + k, pl.ds(start, size)] for k in range(2)], y, start, size, True)

    def m1(slot, yy, start, size):
        m1_step([a1[slot, k, pl.ds(start, size)] for k in range(2)], yy, start, size, False)

    yrel = [wrap(y - 1), wrap(y + 1), wrap(y + 2)]

    def rs1_start(j):
        r1s[rows(j)] = acc1[1 - zl, rows(j)].astype(jnp.bfloat16)
        send(r1s.at[rows(j)], r1r.at[rows(j)], r1ss.at[j], r1rs.at[j], zp)

    def f_start(j):
        arrived(r1r.at[rows(j)], r1ss.at[j], r1rs.at[j])
        total = acc1[zl, rows(j)] + r1r[rows(j)].astype(jnp.float32)
        fa[0, rows(j)] = blocks_masked(total, fm_ref, j)
        for d in range(2):
            send(fa.at[0, rows(j)], fa.at[1 + d, rows(j)], fs.at[d, j], fr.at[d, j], yd[d])

    def f_forward(j):
        for d in range(2):
            arrived(fa.at[1 + d, rows(j)], fs.at[d, j], fr.at[d, j])
        d = j % 2
        send(fa.at[1 + d, rows(j)], fa.at[3, rows(j)], ffs.at[j], ffr.at[j], yd[d])

    def f_opp(j):
        arrived(fa.at[3, rows(j)], ffs.at[j], ffr.at[j])

    def diagonal(h):
        at = pl.multiple_of(core * ROWS + h * HALF, HALF)
        square = acc1[zh, rows(h, HALF), pl.ds(at, HALF)]
        r = lax.broadcasted_iota(jnp.int32, (HALF, HALF), 0)
        c = lax.broadcasted_iota(jnp.int32, (HALF, HALF), 1)
        return jnp.sum(jnp.where(r == c, square, 0.0))

    stages = [
        (core, 2, lambda i: dev(c_=lax.rem(core + i, 2))),
        (z, 4, lambda i: dev(z_=lax.rem(z + i, 4))),
        (y, 4, lambda i: dev(y_=lax.rem(y + i, 4))),
        (x, 4, lambda i: dev(x_=lax.rem(x + i, 4))),
    ]

    def e_send(st):
        me, n, target = stages[st]
        for i in range(1, n):
            send(eb.at[st, me], eb.at[st, me], es.at[st, i], er.at[st, i], target(i))

    def e_sum(st):
        me, n, _ = stages[st]
        for i in range(1, n):
            arrived(eb.at[st, lax.rem(me + n - i, n)], es.at[st, i], er.at[st, i])
        total = eb[st, 0]
        for i in range(1, n):
            total = total + eb[st, i]
        return total

    def e_step(st):
        total = e_sum(st)
        eb[st + 1, stages[st + 1][0]] = total
        e_send(st + 1)

    def m2(t, yy, slot, start, size, first):
        span = pl.ds(start, size)

        for n in range(COLS // NTILE):
            d = jnp.dot(fa[slot, span], b2[t, yy, :, ncols(n)], preferred_element_type=jnp.float32)
            if first:
                acc2[t, span, ncols(n)] = d
            else:
                acc2[t, span, ncols(n)] += d

    def m2_half(h, xx, first):
        gap = wrap(xx - y)
        slot = jnp.where(gap == 0, 0, jnp.where(gap == 3, 1, jnp.where(gap == 1, 2, 3)))

        for n in range(COLS // NTILE):
            d = jnp.zeros((ROWS, NTILE), jnp.float32)
            for c in range(2):
                at = pl.ds(c * ROWS + h * HALF, HALF)
                d += jnp.dot(fa[slot, :, at], b2[1, xx, at, ncols(n)], preferred_element_type=jnp.float32)
            if first:
                acc2[1, :, ncols(n)] = d
            else:
                acc2[1, :, ncols(n)] += d

    def rs2_start(j):
        r2s[rows(j)] = acc2[0, rows(j)].astype(jnp.bfloat16)
        send(r2s.at[rows(j)], r2r.at[rows(j)], r2ss.at[j], r2rs.at[j], z2)

    for j in (1, 2):
        p_mask(j)
    two, three = 2 * CHUNK, 3 * CHUNK
    z_start(1)
    yb_step()
    z_step(0)
    send_a(n1, k1, 0, 0)
    z_step(1)
    z_late(0)
    z_start(2)
    send_a(n1, k1, 0, 1)
    yb_opp()
    z_start(3)
    for i in range(3):
        yz_start_outer(i)
    n2_far(0)
    s_step(0)
    n2_own(0)
    n2_far(1)
    s_step(1)
    z_late(1)
    n2_own(1)
    z_step(2)
    a_forward(k2, 1, 0)
    a_forward(k1, 0, 0)
    b_start(2)
    s_opp(1)
    z_step(3)
    for i in range(3):
        yz_start_inner(i)
    s_opp(0)
    a_forward(k1, 0, 1)
    a_forward(k2, 1, 1)
    for i in range(3):
        yz_relay(i)
    b_start(0)
    z_late(2)
    n2_far(2)
    n2_own(2)
    for i in range(4):
        for h in range(2):
            s_mate(i, h)
    z_far(3)
    a_opp(0)
    m1_own(0, HALF)
    z_late(3)
    a_opp(1)
    send_a(n1, k1, 0, 2)
    b_start(1)
    m1(2, yrel[2], 0, HALF)
    m1(0, yrel[0], 0, HALF)
    m1(1, yrel[1], 0, HALF)
    rs1_start(0)
    a_forward(k2, 1, 2)
    a_forward(k1, 0, 2)
    rs1_start(1)
    m1_own(two, CHUNK)
    m1(0, yrel[0], two, CHUNK)
    m1(1, yrel[1], two, CHUNK)
    f_start(0)
    f_start(1)
    a_opp(2)
    m1_own(three, CHUNK)
    b_step(0)
    m1(2, yrel[2], two, CHUNK)
    rs1_start(2)
    b_step(1)
    b_step(2)
    for i in range(3):
        yz_arrived(i)
        m1(i, yrel[i], three, CHUNK)
    f_forward(0)
    f_forward(1)
    f_start(2)
    rs1_start(3)
    trace = jnp.where(x == y, diagonal(0) + diagonal(1), 0.0)
    eb[0, core] = jnp.full((8, 128), trace, jnp.float32)
    e_send(0)
    b_start(3)
    b_opp(0)
    for i in range(4):
        b_mate(0, i)
    e_step(0)
    f_opp(0)
    b_opp(1)
    f_start(3)
    f_opp(1)
    for i in range(4):
        b_mate(1, i)
    m2(0, y, 0, 0, HALF, True)
    for i in range(2):
        m2(0, yrel[i], 1 + i, 0, HALF, False)
    m2(0, yrel[2], 3, 0, HALF, False)
    rs2_start(1)
    f_forward(2)
    rs2_start(0)
    f_forward(3)
    b_opp(2)
    e_step(1)
    m2(0, y, 0, three, CHUNK, True)
    for i in range(2):
        m2(0, yrel[i], 1 + i, three, CHUNK, False)
    m2(0, y, 0, two, CHUNK, True)
    for i in range(2):
        m2(0, yrel[i], 1 + i, two, CHUNK, False)
    f_opp(2)
    m2(0, yrel[2], 3, two, CHUNK, False)
    rs2_start(2)
    f_opp(3)
    b_step(3)
    for i in range(4):
        b_mate(2, i)
    for i in range(4):
        m2_half(0, xrel[i], i == 0)
    e_step(2)
    m2(0, yrel[2], 3, three, CHUNK, False)
    rs2_start(3)
    for i in range(3):
        b_mate(3, i)
        m2_half(1, xrel[i], False)
    b_opp(3)
    b_mate(3, 3)
    m2_half(1, xrel[3], False)
    e_ref[0, 0] = jnp.max(e_sum(3))
    for j in range(4):
        arrived(r2r.at[rows(j)], r2ss.at[j], r2rs.at[j])
        total = acc2[1, rows(j)] + r2r[rows(j)].astype(jnp.float32)
        o_ref[rows(j)] = blocks_masked(total, fm_ref, j)
    for cp in sent:
        cp.wait_send()
    for i in range(3):
        yz_sent(i)
    for j in range(4):
        z_sent(j)


def shards(density, intersection, density_mask, intersection_mask, filter_mask):
    dma = pltpu.SemaphoreType.DMA
    bf16, f32 = jnp.bfloat16, jnp.float32
    vmem, smem = pl.BlockSpec(memory_space=pltpu.VMEM), pl.BlockSpec(memory_space=pltpu.SMEM)
    psp, electrons = pl.pallas_call(
        kernel,
        out_shape=(jax.ShapeDtypeStruct((ROWS, COLS), bf16), jax.ShapeDtypeStruct((1, 1), f32)),
        in_specs=[smem] * 3 + [vmem] * 2,
        out_specs=(vmem, smem),
        scratch_shapes=[
            pltpu.VMEM((4, ROWS, COLS), bf16),
            pltpu.VMEM((3, CHUNK, COLS), bf16),
            pltpu.VMEM((3, CHUNK, COLS), bf16),
            pltpu.VMEM((3, 2, ROWS, COLS), bf16),
            pltpu.VMEM((4, 2 * ROWS, COLS), bf16),
            pltpu.VMEM((2, 4, 2 * ROWS, COLS), bf16),
            pltpu.VMEM((4, ROWS, COLS), bf16),
            pltpu.VMEM((2, ROWS, COLS), f32),
            pltpu.VMEM((2, ROWS, COLS), f32),
            pltpu.VMEM((ROWS, COLS), bf16),
            pltpu.VMEM((ROWS, COLS), bf16),
            pltpu.VMEM((ROWS, COLS), bf16),
            pltpu.VMEM((ROWS, COLS), bf16),
            pltpu.VMEM((4, 4, 8, 128), f32),
            dma((2, 4)), dma((2, 4)), dma((4,)), dma((4,)),
            dma((2, 2, 4)), dma((2, 2, 4)), dma((2, 4)), dma((2, 4)),
            dma((3,)), dma((3,)), dma((2, 3)), dma((2, 3)),
            dma((2, 2)), dma((2, 2)), dma((2, 2)), dma((2, 2)), dma((4, 2)), dma((4, 2)),
            dma((4, 2)), dma((4, 2)), dma((4, 2)), dma((4, 2)), dma((4, 4)), dma((4, 4)),
            dma((4,)), dma((4,)),
            dma((2, 4)), dma((2, 4)), dma((4,)), dma((4,)),
            dma((4,)), dma((4,)),
            dma((4, 4)), dma((4, 4)),
        ],
        compiler_params=pltpu.CompilerParams(
            collective_id=0, has_side_effects=True, vmem_limit_bytes=62 * 2**20
        ),
        cost_estimate=pl.CostEstimate(flops=17179869184, bytes_accessed=3 * 2**20, transcendentals=0),
    )(density_mask, intersection_mask, filter_mask, density, intersection)
    return psp, electrons.reshape(())


def solution(mesh):
    placed = (P("row", "col"),) * 5
    return jax.shard_map(
        shards, mesh=mesh, in_specs=placed, out_specs=(P("row", "col"), P()), check_vma=False
    )
```

```python
import jax
import jax.numpy as jnp
from jax import lax
from jax.experimental import pallas as pl
from jax.experimental.pallas import tpu as pltpu
from jax.sharding import PartitionSpec as P

BLOCK = 128
ROWS = 512
COLS = 1024
CHUNK = 128
HALF = 256
NTILE = 512
MESH = pl.DeviceIdType.MESH


def kernel(
    dm_ref, im_ref, fm_ref, p_hbm, s_hbm, o_hbm, e_ref,
    p_ref, s_ref, o_ref, pz, yb, yf, a1, s1, b2, fa, acc1, acc2, r1s, r1r, r2s, r2r, eb,
    zs, zr, zfs, zfr, ys, yr, yfs, yfr, ybs, ybr, yzs, yzr, ss, sr, sfs, sfr, sds, sdr,
    bs, br, bfs, bfr, bds, bdr, r1ss, r1rs, fs, fr, ffs, ffr, r2ss, r2rs, es, er, ps, sl, os,
):
    def load(hbm, ref, sems, j):
        span = pl.ds(j * CHUNK, CHUNK)
        return pltpu.make_async_copy(hbm.at[span], ref.at[span], sems.at[j])

    for j in (3, 0, 1, 2):
        load(p_hbm, p_ref, ps, j).start()
    for j in range(4):
        load(s_hbm, s_ref, sl, j).start()

    row = lax.axis_index("row")
    col = lax.axis_index("col")
    core = lax.rem(row, 2)
    zl = lax.rem(row // 2, 2)
    x = row // 4
    zh = lax.rem(col, 2)
    y = col // 2
    z = 2 * zh + zl

    def wrap(v):
        return lax.rem(v + 4, 4)

    def dev(x_=x, y_=y, z_=z, c_=core):
        return {"row": x_ * 4 + lax.rem(z_, 2) * 2 + c_, "col": y_ * 2 + z_ // 2}

    xs = [dev(x_=wrap(x + 1)), dev(x_=wrap(x - 1))]
    yd = [dev(y_=wrap(y + 1)), dev(y_=wrap(y - 1))]
    zd = [dev(z_=wrap(z + 1)), dev(z_=wrap(z - 1))]
    x2, y2, z2 = dev(x_=wrap(x + 2)), dev(y_=wrap(y + 2)), dev(z_=wrap(z + 2))
    zp = dev(z_=2 * zh + 1 - zl)
    mate = dev(c_=1 - core)
    xfrom = [wrap(x - 1), wrap(x + 1)]

    peers = xs + yd + zd + [x2, y2, z2, mate]
    barrier = pltpu.get_barrier_semaphore()
    for d in peers:
        pl.semaphore_signal(barrier, inc=1, device_id=d, device_id_type=MESH)
    pl.semaphore_wait(barrier, len(peers))

    sent, late = [], []

    def copy(src, dst, ssem, rsem, device):
        return pltpu.make_async_remote_copy(
            src_ref=src, dst_ref=dst, send_sem=ssem, recv_sem=rsem,
            device_id=device, device_id_type=MESH,
        )

    def send(src, dst, ssem, rsem, device):
        cp = copy(src, dst, ssem, rsem, device)
        cp.start()
        sent.append(cp)

    def arrived(ref, ssem, rsem):
        copy(ref, ref, ssem, rsem, mate).wait_recv()

    def rows(j, n=CHUNK):
        return pl.ds(j * n, n)

    def blocks_masked(val, mask_ref, i):
        parts = []
        for b in range(COLS // BLOCK):
            keep = jnp.full((BLOCK, BLOCK), mask_ref[i, b], jnp.int32) != 0
            part = val[:, b * BLOCK:(b + 1) * BLOCK].astype(jnp.float32)
            parts.append(jnp.where(keep, part, 0.0))
        return jnp.concatenate(parts, axis=1).astype(jnp.bfloat16)

    n1, k1 = 1 + zl, 1 - zl
    n2, k2 = 3 * zl, zl

    def send_a(n, k, kk, j):
        src = pz.at[n, rows(j)]
        for d in range(2):
            send(src, a1.at[d, k, rows(j)], ys.at[d, kk, j], yr.at[d, k, j], yd[d])

    own_in_a = zh == zl
    inside = zh != zl

    nl = jnp.where(own_in_a, 2 - zl, 3 - 3 * zl)

    def zdev(v):
        return dev(z_=v)

    def z_copies(j):
        src = pz.at[z, rows(j)]
        inner = [
            copy(src, src, zs.at[0, j], zr.at[0, j], zdev(3 - z)),
            copy(src, src, zs.at[1, j], zr.at[0, j], zdev(nl)),
        ]
        outer = copy(src, src, zs.at[0, j], zr.at[1, j], zdev(n1))
        return inner, outer

    def z_start(j):
        inner, outer = z_copies(j)

        @pl.when(own_in_a)
        def _():
            outer.start()

        @pl.when(inside)
        def _():
            for cp in inner:
                cp.start()

    def z_step(j):
        arrived(pz.at[n1, rows(j)], zs.at[0, j], zr.at[0, j])
        @pl.when(inside)
        def _():
            arrived(pz.at[nl, rows(j)], zs.at[0, j], zr.at[1, j])

        src = pz.at[jnp.where(own_in_a, n1, nl), rows(j)]
        send(src, src, zfs.at[j], zfr.at[j], zdev(3 - z))

    def z_far(j):
        @pl.when(inside)
        def _():
            arrived(pz.at[n2, rows(j)], zfs.at[j], zfr.at[j])

    def z_late(j):
        @pl.when(own_in_a)
        def _():
            arrived(pz.at[nl, rows(j)], zfs.at[j], zfr.at[j])

    def z_sent(j):
        inner, outer = z_copies(j)

        @pl.when(own_in_a)
        def _():
            outer.wait_send()

        @pl.when(inside)
        def _():
            for cp in inner:
                cp.wait_send()

    def n2_copies(j):
        src = pz.at[n2, rows(j)]
        return [copy(src, a1.at[d, k2, rows(j)], ys.at[d, 1, j], yr.at[d, k2, j], yd[d]) for d in range(2)]

    def n2_own(j):
        @pl.when(own_in_a)
        def _():
            for cp in n2_copies(j):
                cp.start()

    def n2_far(j):
        @pl.when(inside)
        def _():
            arrived(pz.at[n2, rows(j)], zfs.at[j], zfr.at[j])
            for cp in n2_copies(j):
                cp.start()

        sent.extend(n2_copies(j))

    LAST = 3

    def yb_start():
        for d in range(2):
            send(pz.at[z, rows(LAST)], yb.at[d], ybs.at[d], ybr.at[d], yd[d])

    def yb_step():
        for d in range(2):
            arrived(yb.at[d], ybs.at[d], ybr.at[d])
        for d in range(2):
            part = pl.ds(d * (CHUNK // 2), CHUNK // 2)
            send(yb.at[d, part], yb.at[2, part], yfs.at[d, LAST], yfr.at[d, LAST], yd[d])

    def yb_opp():
        for d in range(2):
            part = pl.ds(d * (CHUNK // 2), CHUNK // 2)
            arrived(yb.at[2, part], yfs.at[d, LAST], yfr.at[d, LAST])

    def yz_copies(i):
        dst = a1.at[i, zl, rows(LAST)]
        near = [
            copy(yb.at[i], dst, yzs.at[0, i], yzr.at[0, i], zdev(3 - z)),
            copy(yb.at[i], dst, yzs.at[1, i], yzr.at[0, i], zdev(nl)),
        ]
        far = copy(yb.at[i], yf.at[i], yzs.at[0, i], yzr.at[1, i], zdev(3 - z))
        return near, far

    def yz_start_outer(i):
        @pl.when(own_in_a)
        def _():
            yz_copies(i)[1].start()
            a1[i, zl, rows(LAST)] = yb[i]

    def yz_start_inner(i):
        @pl.when(inside)
        def _():
            for cp in yz_copies(i)[0]:
                cp.start()

    def yz_pass(i):
        return copy(yf.at[i], a1.at[i, 1 - zl, rows(LAST)], yzs.at[1, i], yzr.at[1, i], zdev(n1))

    def yz_relay(i):
        @pl.when(own_in_a)
        def _():
            arrived(yf.at[i], yzs.at[0, i], yzr.at[1, i])
            yz_pass(i).start()

    def yz_arrived(i):
        arrived(a1.at[i, k1, rows(LAST)], yzs.at[0, i], yzr.at[0, i])

        @pl.when(inside)
        def _():
            arrived(a1.at[i, k2, rows(LAST)], yzs.at[0, i], yzr.at[1, i])

    def yz_sent(i):
        near, far = yz_copies(i)

        @pl.when(own_in_a)
        def _():
            far.wait_send()
            yz_pass(i).wait_send()

        @pl.when(inside)
        def _():
            for cp in near:
                cp.wait_send()

    def p_mask(j):
        load(p_hbm, p_ref, ps, j).wait()
        pz[z, rows(j)] = blocks_masked(p_ref[rows(j)], dm_ref, j)

    p_mask(LAST)
    yb_start()
    p_mask(0)
    z_start(0)

    def s_piece(xx, cc, h):
        return s1.at[xx, pl.ds(pl.multiple_of(cc * ROWS + h * HALF, HALF), HALF)]

    for h in range(2):
        for i in range(2):
            j = 2 * h + i
            load(s_hbm, s_ref, sl, j).wait()
            s1[x, pl.ds(pl.multiple_of(core * ROWS + j * CHUNK, CHUNK), CHUNK)] = blocks_masked(
                s_ref[rows(j)], im_ref, j)
        src = s_piece(x, core, h)
        for d in range(2):
            send(src, src, ss.at[d, h], sr.at[d, h], xs[d])
        send(src, src, sds.at[0, h], sdr.at[0, h], mate)

    def s_part(xx, h, d):
        return s1.at[xx, pl.ds(pl.multiple_of(core * ROWS + h * HALF + d * CHUNK, CHUNK), CHUNK)]

    def s_step(h):
        for d in range(2):
            src = s_piece(xfrom[d], core, h)
            arrived(src, ss.at[d, h], sr.at[d, h])
            part = s_part(xfrom[d], h, d)
            send(part, part, sfs.at[d, h], sfr.at[d, h], xs[d])
            send(src, src, sds.at[1 + d, h], sdr.at[1 + d, h], mate)

    def s_opp(h):
        for d in range(2):
            arrived(s_part(wrap(x + 2), h, d), sfs.at[d, h], sfr.at[d, h])
        src = s_piece(wrap(x + 2), core, h)
        send(src, src, sds.at[3, h], sdr.at[3, h], mate)

    def s_mate(i, h):
        xx = [x, xfrom[0], xfrom[1], wrap(x + 2)][i]
        arrived(s_piece(xx, 1 - core, h), sds.at[i, h], sdr.at[i, h])

    tile = [2 - zh, 3 * zh]

    def b_rows(p, xx, cc, off=0, n=HALF):
        return b2.at[p // 2, xx, pl.ds(pl.multiple_of(cc * ROWS + (p % 2) * HALF + off, n), n)]

    def b_start(p):
        src, dst = pz.at[tile[p // 2], rows(p % 2, HALF)], b_rows(p, x, core)
        for d in range(2):
            send(src, dst, bs.at[p, d], br.at[p, d], xs[d])
        send(src, dst, bds.at[p, 0], bdr.at[p, 0], mate)
        dst[...] = src[...]

    def b_step(p):
        for d in range(2):
            src = b_rows(p, xfrom[d], core)
            arrived(src, bs.at[p, d], br.at[p, d])
            part = b_rows(p, xfrom[d], core, d * CHUNK, CHUNK)
            send(part, part, bfs.at[p, d], bfr.at[p, d], xs[d])
            send(src, src, bds.at[p, 1 + d], bdr.at[p, 1 + d], mate)

    def b_opp(p):
        for d in range(2):
            arrived(b_rows(p, wrap(x + 2), core, d * CHUNK, CHUNK), bfs.at[p, d], bfr.at[p, d])
        src = b_rows(p, wrap(x + 2), core)
        send(src, src, bds.at[p, 3], bdr.at[p, 3], mate)

    xrel = [x, xfrom[0], xfrom[1], wrap(x + 2)]

    def b_mate(p, i):
        arrived(b_rows(p, xrel[i], 1 - core), bds.at[p, i], bdr.at[p, i])

    def a_forward(k, kk, j):
        for d in range(2):
            arrived(a1.at[d, k, rows(j)], ys.at[d, kk, j], yr.at[d, k, j])
        src = a1.at[k, k, rows(j)]
        send(src, a1.at[2, k, rows(j)], yfs.at[k, j], yfr.at[k, j], dev(y_=wrap(y + 1 - 2 * k)))

    def a_opp(j):
        for d in range(2):
            arrived(a1.at[2, d, rows(j)], yfs.at[d, j], yfr.at[d, j])

    def ncols(n):
        return pl.ds(n * NTILE, NTILE)

    def m1_step(left, yy, start, size, first):
        left = jnp.concatenate(left, axis=0)
        for n in range(COLS // NTILE):
            d = jnp.dot(left, s1[yy, :, ncols(n)], preferred_element_type=jnp.float32)
            for k in range(2):
                span, part = pl.ds(start, size), d[k * size:(k + 1) * size]
                if first:
                    acc1[k, span, ncols(n)] = part
                else:
                    acc1[k, span, ncols(n)] += part

    def m1_own(start, size):
        m1_step([pz[2 * zl + k, pl.ds(start, size)] for k in range(2)], y, start, size, True)

    def m1(slot, yy, start, size):
        m1_step([a1[slot, k, pl.ds(start, size)] for k in range(2)], yy, start, size, False)

    yrel = [wrap(y - 1), wrap(y + 1), wrap(y + 2)]

    def rs1_start(j):
        r1s[rows(j)] = acc1[1 - zl, rows(j)].astype(jnp.bfloat16)
        send(r1s.at[rows(j)], r1r.at[rows(j)], r1ss.at[j], r1rs.at[j], zp)

    def f_start(j):
        arrived(r1r.at[rows(j)], r1ss.at[j], r1rs.at[j])
        total = acc1[zl, rows(j)] + r1r[rows(j)].astype(jnp.float32)
        fa[0, rows(j)] = blocks_masked(total, fm_ref, j)
        for d in range(2):
            send(fa.at[0, rows(j)], fa.at[1 + d, rows(j)], fs.at[d, j], fr.at[d, j], yd[d])

    def f_forward(j):
        for d in range(2):
            arrived(fa.at[1 + d, rows(j)], fs.at[d, j], fr.at[d, j])
        d = j % 2
        send(fa.at[1 + d, rows(j)], fa.at[3, rows(j)], ffs.at[j], ffr.at[j], yd[d])

    def f_opp(j):
        arrived(fa.at[3, rows(j)], ffs.at[j], ffr.at[j])

    def diagonal(h):
        at = pl.multiple_of(core * ROWS + h * HALF, HALF)
        square = acc1[zh, rows(h, HALF), pl.ds(at, HALF)]
        r = lax.broadcasted_iota(jnp.int32, (HALF, HALF), 0)
        c = lax.broadcasted_iota(jnp.int32, (HALF, HALF), 1)
        return jnp.sum(jnp.where(r == c, square, 0.0))

    stages = [
        (core, 2, lambda i: dev(c_=lax.rem(core + i, 2))),
        (z, 4, lambda i: dev(z_=lax.rem(z + i, 4))),
        (y, 4, lambda i: dev(y_=lax.rem(y + i, 4))),
        (x, 4, lambda i: dev(x_=lax.rem(x + i, 4))),
    ]

    def e_send(st):
        me, n, target = stages[st]
        for i in range(1, n):
            send(eb.at[st, me], eb.at[st, me], es.at[st, i], er.at[st, i], target(i))

    def e_sum(st):
        me, n, _ = stages[st]
        for i in range(1, n):
            arrived(eb.at[st, lax.rem(me + n - i, n)], es.at[st, i], er.at[st, i])
        total = eb[st, 0]
        for i in range(1, n):
            total = total + eb[st, i]
        return total

    def e_step(st):
        total = e_sum(st)
        eb[st + 1, stages[st + 1][0]] = total
        e_send(st + 1)

    def m2(t, yy, slot, start, size, first):
        span = pl.ds(start, size)

        for n in range(COLS // NTILE):
            d = jnp.dot(fa[slot, span], b2[t, yy, :, ncols(n)], preferred_element_type=jnp.float32)
            if first:
                acc2[t, span, ncols(n)] = d
            else:
                acc2[t, span, ncols(n)] += d

    def m2_half(h, xx, first):
        gap = wrap(xx - y)
        slot = jnp.where(gap == 0, 0, jnp.where(gap == 3, 1, jnp.where(gap == 1, 2, 3)))

        for n in range(COLS // NTILE):
            d = jnp.zeros((ROWS, NTILE), jnp.float32)
            for c in range(2):
                at = pl.ds(c * ROWS + h * HALF, HALF)
                d += jnp.dot(fa[slot, :, at], b2[1, xx, at, ncols(n)], preferred_element_type=jnp.float32)
            if first:
                acc2[1, :, ncols(n)] = d
            else:
                acc2[1, :, ncols(n)] += d

    def rs2_start(j):
        r2s[rows(j)] = acc2[0, rows(j)].astype(jnp.bfloat16)
        send(r2s.at[rows(j)], r2r.at[rows(j)], r2ss.at[j], r2rs.at[j], z2)
        late.append(sent.pop())

    for j in (1, 2):
        p_mask(j)
    two, three = 2 * CHUNK, 3 * CHUNK
    z_start(1)
    yb_step()
    z_step(0)
    send_a(n1, k1, 0, 0)
    z_step(1)
    z_late(0)
    z_start(2)
    send_a(n1, k1, 0, 1)
    yb_opp()
    z_start(3)
    for i in range(3):
        yz_start_outer(i)
    n2_far(0)
    s_step(0)
    n2_own(0)
    n2_far(1)
    s_step(1)
    z_late(1)
    n2_own(1)
    z_step(2)
    a_forward(k2, 1, 0)
    a_forward(k1, 0, 0)
    b_start(2)
    s_opp(1)
    z_step(3)
    for i in range(3):
        yz_start_inner(i)
    s_opp(0)
    a_forward(k1, 0, 1)
    a_forward(k2, 1, 1)
    for i in range(3):
        yz_relay(i)
    b_start(0)
    z_late(2)
    n2_far(2)
    n2_own(2)
    for i in range(4):
        for h in range(2):
            s_mate(i, h)
    z_far(3)
    a_opp(0)
    m1_own(0, HALF)
    z_late(3)
    a_opp(1)
    send_a(n1, k1, 0, 2)
    b_start(1)
    m1(2, yrel[2], 0, HALF)
    m1(0, yrel[0], 0, HALF)
    m1(1, yrel[1], 0, HALF)
    rs1_start(0)
    a_forward(k2, 1, 2)
    a_forward(k1, 0, 2)
    rs1_start(1)
    m1_own(two, CHUNK)
    m1(0, yrel[0], two, CHUNK)
    m1(1, yrel[1], two, CHUNK)
    f_start(0)
    f_start(1)
    a_opp(2)
    m1_own(three, CHUNK)
    b_step(0)
    m1(2, yrel[2], two, CHUNK)
    rs1_start(2)
    b_step(1)
    b_step(2)
    for i in range(3):
        yz_arrived(i)
        m1(i, yrel[i], three, CHUNK)
    f_forward(0)
    f_forward(1)
    f_start(2)
    rs1_start(3)
    trace = jnp.where(x == y, diagonal(0) + diagonal(1), 0.0)
    eb[0, core] = jnp.full((8, 128), trace, jnp.float32)
    e_send(0)
    b_start(3)
    b_opp(0)
    for i in range(4):
        b_mate(0, i)
    e_step(0)
    f_opp(0)
    b_opp(1)
    f_start(3)
    f_opp(1)
    for i in range(4):
        b_mate(1, i)
    m2(0, y, 0, 0, HALF, True)
    for i in range(2):
        m2(0, yrel[i], 1 + i, 0, HALF, False)
    m2(0, yrel[2], 3, 0, HALF, False)
    rs2_start(1)
    f_forward(2)
    rs2_start(0)
    f_forward(3)
    b_opp(2)
    e_step(1)
    m2(0, y, 0, three, CHUNK, True)
    for i in range(2):
        m2(0, yrel[i], 1 + i, three, CHUNK, False)
    m2(0, y, 0, two, CHUNK, True)
    for i in range(2):
        m2(0, yrel[i], 1 + i, two, CHUNK, False)
    f_opp(2)
    m2(0, yrel[2], 3, two, CHUNK, False)
    rs2_start(2)
    f_opp(3)
    b_step(3)
    for i in range(4):
        b_mate(2, i)
    for i in range(4):
        m2_half(0, xrel[i], i == 0)
    e_step(2)
    m2(0, yrel[2], 3, three, CHUNK, False)
    rs2_start(3)
    for i in range(3):
        b_mate(3, i)
        m2_half(1, xrel[i], False)
    b_opp(3)
    b_mate(3, 3)
    m2_half(1, xrel[3], False)
    e_ref[0, 0] = jnp.max(e_sum(3))
    for cp in sent:
        cp.wait_send()
    for i in range(3):
        yz_sent(i)
    for j in range(4):
        z_sent(j)

    def store(j):
        return pltpu.make_async_copy(o_ref.at[rows(j)], o_hbm.at[rows(j)], os.at[j])

    for j in range(4):
        arrived(r2r.at[rows(j)], r2ss.at[j], r2rs.at[j])
        total = acc2[1, rows(j)] + r2r[rows(j)].astype(jnp.float32)
        o_ref[rows(j)] = blocks_masked(total, fm_ref, j)
        store(j).start()
    for cp in late:
        cp.wait_send()
    for j in range(4):
        store(j).wait()


def place(psp_ref, trace_ref, to_ref, to_trace_ref, held, in_sems, out_sems):
    spans = [pl.ds(i * 64, 64) for i in range(8)]
    loads = [pltpu.make_async_copy(psp_ref.at[s], held.at[s], in_sems.at[i]) for i, s in enumerate(spans)]
    stores = [pltpu.make_async_copy(held.at[s], to_ref.at[s], out_sems.at[i]) for i, s in enumerate(spans)]
    for cp in loads:
        cp.start()
    to_trace_ref[0, 0] = trace_ref[0, 0]
    for load, store in zip(loads, stores):
        load.wait()
        store.start()
    for cp in stores:
        cp.wait()


def shards(density, intersection, density_mask, intersection_mask, filter_mask):
    dma = pltpu.SemaphoreType.DMA
    bf16, f32 = jnp.bfloat16, jnp.float32
    hbm, smem = pl.BlockSpec(memory_space=pl.ANY), pl.BlockSpec(memory_space=pltpu.SMEM)
    psp, electrons = pl.pallas_call(
        kernel,
        out_shape=(jax.ShapeDtypeStruct((ROWS, COLS), bf16), jax.ShapeDtypeStruct((1, 1), f32)),
        in_specs=[smem] * 3 + [hbm] * 2,
        out_specs=(hbm, smem),
        scratch_shapes=[
            pltpu.VMEM((ROWS, COLS), bf16),
            pltpu.VMEM((ROWS, COLS), bf16),
            pltpu.VMEM((ROWS, COLS), bf16),
            pltpu.VMEM((4, ROWS, COLS), bf16),
            pltpu.VMEM((3, CHUNK, COLS), bf16),
            pltpu.VMEM((3, CHUNK, COLS), bf16),
            pltpu.VMEM((3, 2, ROWS, COLS), bf16),
            pltpu.VMEM((4, 2 * ROWS, COLS), bf16),
            pltpu.VMEM((2, 4, 2 * ROWS, COLS), bf16),
            pltpu.VMEM((4, ROWS, COLS), bf16),
            pltpu.VMEM((2, ROWS, COLS), f32),
            pltpu.VMEM((2, ROWS, COLS), f32),
            pltpu.VMEM((ROWS, COLS), bf16),
            pltpu.VMEM((ROWS, COLS), bf16),
            pltpu.VMEM((ROWS, COLS), bf16),
            pltpu.VMEM((ROWS, COLS), bf16),
            pltpu.VMEM((4, 4, 8, 128), f32),
            dma((2, 4)), dma((2, 4)), dma((4,)), dma((4,)),
            dma((2, 2, 4)), dma((2, 2, 4)), dma((2, 4)), dma((2, 4)),
            dma((3,)), dma((3,)), dma((2, 3)), dma((2, 3)),
            dma((2, 2)), dma((2, 2)), dma((2, 2)), dma((2, 2)), dma((4, 2)), dma((4, 2)),
            dma((4, 2)), dma((4, 2)), dma((4, 2)), dma((4, 2)), dma((4, 4)), dma((4, 4)),
            dma((4,)), dma((4,)),
            dma((2, 4)), dma((2, 4)), dma((4,)), dma((4,)),
            dma((4,)), dma((4,)),
            dma((4, 4)), dma((4, 4)),
            dma((4,)), dma((4,)), dma((4,)),
        ],
        compiler_params=pltpu.CompilerParams(
            collective_id=0, has_side_effects=True, vmem_limit_bytes=62 * 2**20
        ),
        cost_estimate=pl.CostEstimate(flops=17179869184, bytes_accessed=3 * 2**20, transcendentals=0),
    )(density_mask, intersection_mask, filter_mask, density, intersection)
    psp, electrons = pl.pallas_call(
        place,
        out_shape=(jax.ShapeDtypeStruct((ROWS, COLS), bf16), jax.ShapeDtypeStruct((1, 1), f32)),
        in_specs=[hbm, smem],
        out_specs=(hbm, smem),
        scratch_shapes=[pltpu.VMEM((ROWS, COLS), bf16), dma((8,)), dma((8,))],
    )(psp, electrons)
    return psp, electrons.reshape(())


def solution(mesh):
    placed = (P("row", "col"),) * 5
    return jax.shard_map(
        shards, mesh=mesh, in_specs=placed, out_specs=(P("row", "col"), P()), check_vma=False
    )
```

```python
import jax
import jax.numpy as jnp
from jax import lax
from jax.experimental import pallas as pl
from jax.experimental.pallas import tpu as pltpu
from jax.sharding import PartitionSpec as P

BLOCK = 128
ROWS = 512
COLS = 1024
CHUNK = 128
HALF = 256
NTILE = 512
MESH = pl.DeviceIdType.MESH


def kernel(
    dm_ref, im_ref, fm_ref, p_hbm, s_hbm, o_hbm, e_ref,
    p_ref, s_ref, o_ref, pz, yb, yf, a1, s1, b2, fa, acc1, acc2, r1s, r1r, r2s, r2r, eb,
    zs, zr, zfs, zfr, ys, yr, yfs, yfr, ybs, ybr, yzs, yzr, ss, sr, sfs, sfr, sds, sdr,
    bs, br, bfs, bfr, bds, bdr, r1ss, r1rs, fs, fr, ffs, ffr, r2ss, r2rs, es, er, ps, sl, os,
):
    def load(hbm, ref, sems, j):
        span = pl.ds(j * CHUNK, CHUNK)
        return pltpu.make_async_copy(hbm.at[span], ref.at[span], sems.at[j])

    for j in (3, 0, 1, 2):
        load(p_hbm, p_ref, ps, j).start()
    for j in range(4):
        load(s_hbm, s_ref, sl, j).start()

    row = lax.axis_index("row")
    col = lax.axis_index("col")
    core = lax.rem(row, 2)
    zl = lax.rem(row // 2, 2)
    x = row // 4
    zh = lax.rem(col, 2)
    y = col // 2
    z = 2 * zh + zl

    def wrap(v):
        return lax.rem(v + 4, 4)

    def dev(x_=x, y_=y, z_=z, c_=core):
        return {"row": x_ * 4 + lax.rem(z_, 2) * 2 + c_, "col": y_ * 2 + z_ // 2}

    xs = [dev(x_=wrap(x + 1)), dev(x_=wrap(x - 1))]
    yd = [dev(y_=wrap(y + 1)), dev(y_=wrap(y - 1))]
    zd = [dev(z_=wrap(z + 1)), dev(z_=wrap(z - 1))]
    x2, y2, z2 = dev(x_=wrap(x + 2)), dev(y_=wrap(y + 2)), dev(z_=wrap(z + 2))
    zp = dev(z_=2 * zh + 1 - zl)
    mate = dev(c_=1 - core)
    xfrom = [wrap(x - 1), wrap(x + 1)]

    peers = xs + yd + zd + [x2, y2, z2, mate]
    barrier = pltpu.get_barrier_semaphore()
    for d in peers:
        pl.semaphore_signal(barrier, inc=1, device_id=d, device_id_type=MESH)
    pl.semaphore_wait(barrier, len(peers))

    sent, late = [], []

    def copy(src, dst, ssem, rsem, device):
        return pltpu.make_async_remote_copy(
            src_ref=src, dst_ref=dst, send_sem=ssem, recv_sem=rsem,
            device_id=device, device_id_type=MESH,
        )

    def send(src, dst, ssem, rsem, device):
        cp = copy(src, dst, ssem, rsem, device)
        cp.start()
        sent.append(cp)

    def arrived(ref, ssem, rsem):
        copy(ref, ref, ssem, rsem, mate).wait_recv()

    def rows(j, n=CHUNK):
        return pl.ds(j * n, n)

    def blocks_masked(val, mask_ref, i):
        parts = []
        for b in range(COLS // BLOCK):
            keep = jnp.full((BLOCK, BLOCK), mask_ref[i, b], jnp.int32) != 0
            part = val[:, b * BLOCK:(b + 1) * BLOCK].astype(jnp.float32)
            parts.append(jnp.where(keep, part, 0.0))
        return jnp.concatenate(parts, axis=1).astype(jnp.bfloat16)

    n1, k1 = 1 + zl, 1 - zl
    n2, k2 = 3 * zl, zl

    def send_a(n, k, kk, j):
        src = pz.at[n, rows(j)]
        for d in range(2):
            send(src, a1.at[d, k, rows(j)], ys.at[d, kk, j], yr.at[d, k, j], yd[d])

    own_in_a = zh == zl
    inside = zh != zl

    nl = jnp.where(own_in_a, 2 - zl, 3 - 3 * zl)

    def zdev(v):
        return dev(z_=v)

    def z_copies(j):
        src = pz.at[z, rows(j)]
        inner = [
            copy(src, src, zs.at[0, j], zr.at[0, j], zdev(3 - z)),
            copy(src, src, zs.at[1, j], zr.at[0, j], zdev(nl)),
        ]
        outer = copy(src, src, zs.at[0, j], zr.at[1, j], zdev(n1))
        return inner, outer

    def z_start(j):
        inner, outer = z_copies(j)

        @pl.when(own_in_a)
        def _():
            outer.start()

        @pl.when(inside)
        def _():
            for cp in inner:
                cp.start()

    def z_step(j):
        arrived(pz.at[n1, rows(j)], zs.at[0, j], zr.at[0, j])
        @pl.when(inside)
        def _():
            arrived(pz.at[nl, rows(j)], zs.at[0, j], zr.at[1, j])

        src = pz.at[jnp.where(own_in_a, n1, nl), rows(j)]
        send(src, src, zfs.at[j], zfr.at[j], zdev(3 - z))

    def z_far(j):
        @pl.when(inside)
        def _():
            arrived(pz.at[n2, rows(j)], zfs.at[j], zfr.at[j])

    def z_late(j):
        @pl.when(own_in_a)
        def _():
            arrived(pz.at[nl, rows(j)], zfs.at[j], zfr.at[j])

    def z_sent(j):
        inner, outer = z_copies(j)

        @pl.when(own_in_a)
        def _():
            outer.wait_send()

        @pl.when(inside)
        def _():
            for cp in inner:
                cp.wait_send()

    def n2_copies(j):
        src = pz.at[n2, rows(j)]
        return [copy(src, a1.at[d, k2, rows(j)], ys.at[d, 1, j], yr.at[d, k2, j], yd[d]) for d in range(2)]

    def n2_own(j):
        @pl.when(own_in_a)
        def _():
            for cp in n2_copies(j):
                cp.start()

    def n2_far(j):
        @pl.when(inside)
        def _():
            arrived(pz.at[n2, rows(j)], zfs.at[j], zfr.at[j])
            for cp in n2_copies(j):
                cp.start()

        sent.extend(n2_copies(j))

    LAST = 3

    def yb_start():
        for d in range(2):
            send(pz.at[z, rows(LAST)], yb.at[d], ybs.at[d], ybr.at[d], yd[d])

    def yb_step():
        for d in range(2):
            arrived(yb.at[d], ybs.at[d], ybr.at[d])
        for d in range(2):
            part = pl.ds(d * (CHUNK // 2), CHUNK // 2)
            send(yb.at[d, part], yb.at[2, part], yfs.at[d, LAST], yfr.at[d, LAST], yd[d])

    def yb_opp():
        for d in range(2):
            part = pl.ds(d * (CHUNK // 2), CHUNK // 2)
            arrived(yb.at[2, part], yfs.at[d, LAST], yfr.at[d, LAST])

    def yz_copies(i):
        dst = a1.at[i, zl, rows(LAST)]
        near = [
            copy(yb.at[i], dst, yzs.at[0, i], yzr.at[0, i], zdev(3 - z)),
            copy(yb.at[i], dst, yzs.at[1, i], yzr.at[0, i], zdev(nl)),
        ]
        far = copy(yb.at[i], yf.at[i], yzs.at[0, i], yzr.at[1, i], zdev(3 - z))
        return near, far

    def yz_start_outer(i):
        @pl.when(own_in_a)
        def _():
            yz_copies(i)[1].start()
            a1[i, zl, rows(LAST)] = yb[i]

    def yz_start_inner(i):
        @pl.when(inside)
        def _():
            for cp in yz_copies(i)[0]:
                cp.start()

    def yz_pass(i):
        return copy(yf.at[i], a1.at[i, 1 - zl, rows(LAST)], yzs.at[1, i], yzr.at[1, i], zdev(n1))

    def yz_relay(i):
        @pl.when(own_in_a)
        def _():
            arrived(yf.at[i], yzs.at[0, i], yzr.at[1, i])
            yz_pass(i).start()

    def yz_arrived(i):
        arrived(a1.at[i, k1, rows(LAST)], yzs.at[0, i], yzr.at[0, i])

        @pl.when(inside)
        def _():
            arrived(a1.at[i, k2, rows(LAST)], yzs.at[0, i], yzr.at[1, i])

    def yz_sent(i):
        near, far = yz_copies(i)

        @pl.when(own_in_a)
        def _():
            far.wait_send()
            yz_pass(i).wait_send()

        @pl.when(inside)
        def _():
            for cp in near:
                cp.wait_send()

    def p_mask(j):
        load(p_hbm, p_ref, ps, j).wait()
        pz[z, rows(j)] = blocks_masked(p_ref[rows(j)], dm_ref, j)

    p_mask(LAST)
    yb_start()
    p_mask(0)
    z_start(0)

    def s_piece(xx, cc, h):
        return s1.at[xx, pl.ds(pl.multiple_of(cc * ROWS + h * HALF, HALF), HALF)]

    for h in range(2):
        for i in range(2):
            j = 2 * h + i
            load(s_hbm, s_ref, sl, j).wait()
            s1[x, pl.ds(pl.multiple_of(core * ROWS + j * CHUNK, CHUNK), CHUNK)] = blocks_masked(
                s_ref[rows(j)], im_ref, j)
        src = s_piece(x, core, h)
        for d in range(2):
            send(src, src, ss.at[d, h], sr.at[d, h], xs[d])
        send(src, src, sds.at[0, h], sdr.at[0, h], mate)

    def s_part(xx, h, d):
        return s1.at[xx, pl.ds(pl.multiple_of(core * ROWS + h * HALF + d * CHUNK, CHUNK), CHUNK)]

    def s_step(h):
        for d in range(2):
            src = s_piece(xfrom[d], core, h)
            arrived(src, ss.at[d, h], sr.at[d, h])
            part = s_part(xfrom[d], h, d)
            send(part, part, sfs.at[d, h], sfr.at[d, h], xs[d])
            send(src, src, sds.at[1 + d, h], sdr.at[1 + d, h], mate)

    def s_opp(h):
        for d in range(2):
            arrived(s_part(wrap(x + 2), h, d), sfs.at[d, h], sfr.at[d, h])
        src = s_piece(wrap(x + 2), core, h)
        send(src, src, sds.at[3, h], sdr.at[3, h], mate)

    def s_mate(i, h):
        xx = [x, xfrom[0], xfrom[1], wrap(x + 2)][i]
        arrived(s_piece(xx, 1 - core, h), sds.at[i, h], sdr.at[i, h])

    tile = [2 - zh, 3 * zh]

    def b_rows(p, xx, cc, off=0, n=HALF):
        return b2.at[p // 2, xx, pl.ds(pl.multiple_of(cc * ROWS + (p % 2) * HALF + off, n), n)]

    def b_start(p):
        src, dst = pz.at[tile[p // 2], rows(p % 2, HALF)], b_rows(p, x, core)
        for d in range(2):
            send(src, dst, bs.at[p, d], br.at[p, d], xs[d])
        send(src, dst, bds.at[p, 0], bdr.at[p, 0], mate)
        dst[...] = src[...]

    def b_step(p):
        for d in range(2):
            src = b_rows(p, xfrom[d], core)
            arrived(src, bs.at[p, d], br.at[p, d])
            part = b_rows(p, xfrom[d], core, d * CHUNK, CHUNK)
            send(part, part, bfs.at[p, d], bfr.at[p, d], xs[d])
            send(src, src, bds.at[p, 1 + d], bdr.at[p, 1 + d], mate)

    def b_opp(p):
        for d in range(2):
            arrived(b_rows(p, wrap(x + 2), core, d * CHUNK, CHUNK), bfs.at[p, d], bfr.at[p, d])
        src = b_rows(p, wrap(x + 2), core)
        send(src, src, bds.at[p, 3], bdr.at[p, 3], mate)

    xrel = [x, xfrom[0], xfrom[1], wrap(x + 2)]

    def b_mate(p, i):
        arrived(b_rows(p, xrel[i], 1 - core), bds.at[p, i], bdr.at[p, i])

    def a_forward(k, kk, j):
        for d in range(2):
            arrived(a1.at[d, k, rows(j)], ys.at[d, kk, j], yr.at[d, k, j])
        src = a1.at[k, k, rows(j)]
        send(src, a1.at[2, k, rows(j)], yfs.at[k, j], yfr.at[k, j], dev(y_=wrap(y + 1 - 2 * k)))

    def a_opp(j):
        for d in range(2):
            arrived(a1.at[2, d, rows(j)], yfs.at[d, j], yfr.at[d, j])

    def ncols(n):
        return pl.ds(n * NTILE, NTILE)

    def m1_step(left, yy, start, size, first):
        left = jnp.concatenate(left, axis=0)
        for n in range(COLS // NTILE):
            d = jnp.dot(left, s1[yy, :, ncols(n)], preferred_element_type=jnp.float32)
            for k in range(2):
                span, part = pl.ds(start, size), d[k * size:(k + 1) * size]
                if first:
                    acc1[k, span, ncols(n)] = part
                else:
                    acc1[k, span, ncols(n)] += part

    def m1_own(start, size):
        m1_step([pz[2 * zl + k, pl.ds(start, size)] for k in range(2)], y, start, size, True)

    def m1(slot, yy, start, size):
        m1_step([a1[slot, k, pl.ds(start, size)] for k in range(2)], yy, start, size, False)

    yrel = [wrap(y - 1), wrap(y + 1), wrap(y + 2)]

    def rs1_start(j):
        r1s[rows(j)] = acc1[1 - zl, rows(j)].astype(jnp.bfloat16)
        send(r1s.at[rows(j)], r1r.at[rows(j)], r1ss.at[j], r1rs.at[j], zp)

    def f_start(j):
        arrived(r1r.at[rows(j)], r1ss.at[j], r1rs.at[j])
        total = acc1[zl, rows(j)] + r1r[rows(j)].astype(jnp.float32)
        fa[0, rows(j)] = blocks_masked(total, fm_ref, j)
        for d in range(2):
            send(fa.at[0, rows(j)], fa.at[1 + d, rows(j)], fs.at[d, j], fr.at[d, j], yd[d])

    def f_forward(j):
        for d in range(2):
            arrived(fa.at[1 + d, rows(j)], fs.at[d, j], fr.at[d, j])
        d = j % 2
        send(fa.at[1 + d, rows(j)], fa.at[3, rows(j)], ffs.at[j], ffr.at[j], yd[d])

    def f_opp(j):
        arrived(fa.at[3, rows(j)], ffs.at[j], ffr.at[j])

    def diagonal(h):
        at = pl.multiple_of(core * ROWS + h * HALF, HALF)
        square = acc1[zh, rows(h, HALF), pl.ds(at, HALF)]
        r = lax.broadcasted_iota(jnp.int32, (HALF, HALF), 0)
        c = lax.broadcasted_iota(jnp.int32, (HALF, HALF), 1)
        return jnp.sum(jnp.where(r == c, square, 0.0))

    stages = [
        (core, 2, lambda i: dev(c_=lax.rem(core + i, 2))),
        (z, 4, lambda i: dev(z_=lax.rem(z + i, 4))),
        (y, 4, lambda i: dev(y_=lax.rem(y + i, 4))),
        (x, 4, lambda i: dev(x_=lax.rem(x + i, 4))),
    ]

    def e_send(st):
        me, n, target = stages[st]
        for i in range(1, n):
            send(eb.at[st, me], eb.at[st, me], es.at[st, i], er.at[st, i], target(i))

    def e_sum(st):
        me, n, _ = stages[st]
        for i in range(1, n):
            arrived(eb.at[st, lax.rem(me + n - i, n)], es.at[st, i], er.at[st, i])
        total = eb[st, 0]
        for i in range(1, n):
            total = total + eb[st, i]
        return total

    def e_step(st):
        total = e_sum(st)
        eb[st + 1, stages[st + 1][0]] = total
        e_send(st + 1)

    def m2(t, yy, slot, start, size, first):
        span = pl.ds(start, size)

        for n in range(COLS // NTILE):
            d = jnp.dot(fa[slot, span], b2[t, yy, :, ncols(n)], preferred_element_type=jnp.float32)
            if first:
                acc2[t, span, ncols(n)] = d
            else:
                acc2[t, span, ncols(n)] += d

    def m2_half(h, xx, first):
        gap = wrap(xx - y)
        slot = jnp.where(gap == 0, 0, jnp.where(gap == 3, 1, jnp.where(gap == 1, 2, 3)))

        for n in range(COLS // NTILE):
            d = jnp.zeros((ROWS, NTILE), jnp.float32)
            for c in range(2):
                at = pl.ds(c * ROWS + h * HALF, HALF)
                d += jnp.dot(fa[slot, :, at], b2[1, xx, at, ncols(n)], preferred_element_type=jnp.float32)
            if first:
                acc2[1, :, ncols(n)] = d
            else:
                acc2[1, :, ncols(n)] += d

    def rs2_start(j):
        r2s[rows(j)] = acc2[0, rows(j)].astype(jnp.bfloat16)
        send(r2s.at[rows(j)], r2r.at[rows(j)], r2ss.at[j], r2rs.at[j], z2)
        late.append(sent.pop())

    for j in (1, 2):
        p_mask(j)
    two, three = 2 * CHUNK, 3 * CHUNK
    z_start(1)
    n2_own(0)
    yb_step()
    z_step(0)
    send_a(n1, k1, 0, 0)
    z_step(1)
    send_a(n1, k1, 0, 1)
    n2_far(0)
    s_step(0)
    z_start(2)
    n2_own(1)
    z_late(0)
    yb_opp()
    for i in range(3):
        yz_start_outer(i)
    z_start(3)
    n2_far(1)
    s_step(1)
    a_forward(k2, 1, 0)
    a_forward(k1, 0, 0)
    b_start(2)
    z_step(2)
    s_opp(0)
    a_forward(k2, 1, 1)
    z_step(3)
    a_forward(k1, 0, 1)
    for i in range(3):
        yz_start_inner(i)
    z_late(1)
    for i in range(3):
        yz_relay(i)
    s_opp(1)
    b_start(0)
    n2_own(2)
    send_a(n1, k1, 0, 2)
    for i in range(4):
        for h in range(2):
            s_mate(i, h)
    m1_own(0, HALF)
    a_opp(0)
    a_opp(1)
    z_late(2)
    n2_far(2)
    m1(0, yrel[0], 0, HALF)
    m1(1, yrel[1], 0, HALF)
    m1(2, yrel[2], 0, HALF)
    rs1_start(0)
    z_late(3)
    z_far(3)
    rs1_start(1)
    m1_own(three, CHUNK)
    b_start(1)
    a_forward(k1, 0, 2)
    a_forward(k2, 1, 2)
    m1_own(two, CHUNK)
    f_start(0)
    for i in range(3):
        yz_arrived(i)
        m1(i, yrel[i], three, CHUNK)
    a_opp(2)
    rs1_start(3)
    m1(2, yrel[2], two, CHUNK)
    f_start(1)
    b_step(0)
    m1(0, yrel[0], two, CHUNK)
    m1(1, yrel[1], two, CHUNK)
    b_step(1)
    f_forward(0)
    rs1_start(2)
    trace = jnp.where(x == y, diagonal(0) + diagonal(1), 0.0)
    eb[0, core] = jnp.full((8, 128), trace, jnp.float32)
    e_send(0)
    f_forward(1)
    e_step(0)
    b_opp(0)
    f_start(2)
    b_opp(1)
    b_start(3)
    f_opp(0)
    f_start(3)
    for i in range(4):
        b_mate(0, i)
    f_opp(1)
    for i in range(4):
        b_mate(1, i)
    m2(0, y, 0, 0, HALF, True)
    for i in range(2):
        m2(0, yrel[i], 1 + i, 0, HALF, False)
    m2(0, yrel[2], 3, 0, HALF, False)
    rs2_start(0)
    rs2_start(1)
    f_forward(2)
    m2(0, y, 0, two, CHUNK, True)
    for i in range(2):
        m2(0, yrel[i], 1 + i, two, CHUNK, False)
    b_step(2)
    f_forward(3)
    f_opp(2)
    m2(0, yrel[2], 3, two, CHUNK, False)
    rs2_start(2)
    b_step(3)
    m2(0, y, 0, three, CHUNK, True)
    for i in range(2):
        m2(0, yrel[i], 1 + i, three, CHUNK, False)
    e_step(1)
    b_opp(2)
    f_opp(3)
    m2(0, yrel[2], 3, three, CHUNK, False)
    rs2_start(3)
    e_step(2)
    for i in range(4):
        b_mate(2, i)
    for i in range(4):
        m2_half(0, xrel[i], i == 0)
    b_opp(3)
    for i in range(3):
        b_mate(3, i)
        m2_half(1, xrel[i], False)
    b_mate(3, 3)
    m2_half(1, xrel[3], False)
    e_ref[0, 0] = jnp.max(e_sum(3))
    for cp in sent:
        cp.wait_send()
    for i in range(3):
        yz_sent(i)
    for j in range(4):
        z_sent(j)

    def store(j):
        return pltpu.make_async_copy(o_ref.at[rows(j)], o_hbm.at[rows(j)], os.at[j])

    for j in range(4):
        arrived(r2r.at[rows(j)], r2ss.at[j], r2rs.at[j])
        total = acc2[1, rows(j)] + r2r[rows(j)].astype(jnp.float32)
        o_ref[rows(j)] = blocks_masked(total, fm_ref, j)
        store(j).start()
    for cp in late:
        cp.wait_send()
    for j in range(4):
        store(j).wait()


def place(psp_ref, trace_ref, to_ref, to_trace_ref, held, in_sems, out_sems):
    spans = [pl.ds(i * 64, 64) for i in range(8)]
    loads = [pltpu.make_async_copy(psp_ref.at[s], held.at[s], in_sems.at[i]) for i, s in enumerate(spans)]
    stores = [pltpu.make_async_copy(held.at[s], to_ref.at[s], out_sems.at[i]) for i, s in enumerate(spans)]
    for cp in loads:
        cp.start()
    to_trace_ref[0, 0] = trace_ref[0, 0]
    for load, store in zip(loads, stores):
        load.wait()
        store.start()
    for cp in stores:
        cp.wait()


def shards(density, intersection, density_mask, intersection_mask, filter_mask):
    dma = pltpu.SemaphoreType.DMA
    bf16, f32 = jnp.bfloat16, jnp.float32
    hbm, smem = pl.BlockSpec(memory_space=pl.ANY), pl.BlockSpec(memory_space=pltpu.SMEM)
    psp, electrons = pl.pallas_call(
        kernel,
        out_shape=(jax.ShapeDtypeStruct((ROWS, COLS), bf16), jax.ShapeDtypeStruct((1, 1), f32)),
        in_specs=[smem] * 3 + [hbm] * 2,
        out_specs=(hbm, smem),
        scratch_shapes=[
            pltpu.VMEM((ROWS, COLS), bf16),
            pltpu.VMEM((ROWS, COLS), bf16),
            pltpu.VMEM((ROWS, COLS), bf16),
            pltpu.VMEM((4, ROWS, COLS), bf16),
            pltpu.VMEM((3, CHUNK, COLS), bf16),
            pltpu.VMEM((3, CHUNK, COLS), bf16),
            pltpu.VMEM((3, 2, ROWS, COLS), bf16),
            pltpu.VMEM((4, 2 * ROWS, COLS), bf16),
            pltpu.VMEM((2, 4, 2 * ROWS, COLS), bf16),
            pltpu.VMEM((4, ROWS, COLS), bf16),
            pltpu.VMEM((2, ROWS, COLS), f32),
            pltpu.VMEM((2, ROWS, COLS), f32),
            pltpu.VMEM((ROWS, COLS), bf16),
            pltpu.VMEM((ROWS, COLS), bf16),
            pltpu.VMEM((ROWS, COLS), bf16),
            pltpu.VMEM((ROWS, COLS), bf16),
            pltpu.VMEM((4, 4, 8, 128), f32),
            dma((2, 4)), dma((2, 4)), dma((4,)), dma((4,)),
            dma((2, 2, 4)), dma((2, 2, 4)), dma((2, 4)), dma((2, 4)),
            dma((3,)), dma((3,)), dma((2, 3)), dma((2, 3)),
            dma((2, 2)), dma((2, 2)), dma((2, 2)), dma((2, 2)), dma((4, 2)), dma((4, 2)),
            dma((4, 2)), dma((4, 2)), dma((4, 2)), dma((4, 2)), dma((4, 4)), dma((4, 4)),
            dma((4,)), dma((4,)),
            dma((2, 4)), dma((2, 4)), dma((4,)), dma((4,)),
            dma((4,)), dma((4,)),
            dma((4, 4)), dma((4, 4)),
            dma((4,)), dma((4,)), dma((4,)),
        ],
        compiler_params=pltpu.CompilerParams(
            collective_id=0, has_side_effects=True, vmem_limit_bytes=62 * 2**20
        ),
        cost_estimate=pl.CostEstimate(flops=17179869184, bytes_accessed=3 * 2**20, transcendentals=0),
    )(density_mask, intersection_mask, filter_mask, density, intersection)
    psp, electrons = pl.pallas_call(
        place,
        out_shape=(jax.ShapeDtypeStruct((ROWS, COLS), bf16), jax.ShapeDtypeStruct((1, 1), f32)),
        in_specs=[hbm, smem],
        out_specs=(hbm, smem),
        scratch_shapes=[pltpu.VMEM((ROWS, COLS), bf16), dma((8,)), dma((8,))],
    )(psp, electrons)
    return psp, electrons.reshape(())


def solution(mesh):
    placed = (P("row", "col"),) * 5
    return jax.shard_map(
        shards, mesh=mesh, in_specs=placed, out_specs=(P("row", "col"), P()), check_vma=False
    )
```

```python
import jax
import jax.numpy as jnp
from jax import lax
from jax.experimental import pallas as pl
from jax.experimental.pallas import tpu as pltpu
from jax.sharding import PartitionSpec as P

BLOCK = 128
ROWS = 512
COLS = 1024
CHUNK = 128
HALF = 256
NTILE = 1024
MESH = pl.DeviceIdType.MESH


def kernel(
    dm_ref, im_ref, fm_ref, p_hbm, s_hbm, o_hbm, e_ref,
    p_ref, s_ref, o_ref, pz, yb, yf, a1, s1, b2, fa, acc1, acc2, r1s, r1r, r2s, r2r, eb,
    zs, zr, zfs, zfr, ys, yr, yfs, yfr, ybs, ybr, yzs, yzr, ss, sr, sfs, sfr, sds, sdr,
    bs, br, bfs, bfr, bds, bdr, r1ss, r1rs, fs, fr, ffs, ffr, r2ss, r2rs, es, er, ps, sl, os,
):
    def load(hbm, ref, sems, j):
        span = pl.ds(j * CHUNK, CHUNK)
        return pltpu.make_async_copy(hbm.at[span], ref.at[span], sems.at[j])

    for j in (3, 0, 1, 2):
        load(p_hbm, p_ref, ps, j).start()
    for j in range(4):
        load(s_hbm, s_ref, sl, j).start()

    row = lax.axis_index("row")
    col = lax.axis_index("col")
    core = lax.rem(row, 2)
    zl = lax.rem(row // 2, 2)
    x = row // 4
    zh = lax.rem(col, 2)
    y = col // 2
    z = 2 * zh + zl

    def wrap(v):
        return lax.rem(v + 4, 4)

    def dev(x_=x, y_=y, z_=z, c_=core):
        return {"row": x_ * 4 + lax.rem(z_, 2) * 2 + c_, "col": y_ * 2 + z_ // 2}

    xs = [dev(x_=wrap(x + 1)), dev(x_=wrap(x - 1))]
    yd = [dev(y_=wrap(y + 1)), dev(y_=wrap(y - 1))]
    zd = [dev(z_=wrap(z + 1)), dev(z_=wrap(z - 1))]
    x2, y2, z2 = dev(x_=wrap(x + 2)), dev(y_=wrap(y + 2)), dev(z_=wrap(z + 2))
    zp = dev(z_=2 * zh + 1 - zl)
    mate = dev(c_=1 - core)
    xfrom = [wrap(x - 1), wrap(x + 1)]

    peers = xs + yd + zd + [x2, y2, z2, mate]
    barrier = pltpu.get_barrier_semaphore()
    for d in peers:
        pl.semaphore_signal(barrier, inc=1, device_id=d, device_id_type=MESH)
    pl.semaphore_wait(barrier, len(peers))

    sent, late = [], []

    def copy(src, dst, ssem, rsem, device):
        return pltpu.make_async_remote_copy(
            src_ref=src, dst_ref=dst, send_sem=ssem, recv_sem=rsem,
            device_id=device, device_id_type=MESH,
        )

    def send(src, dst, ssem, rsem, device):
        cp = copy(src, dst, ssem, rsem, device)
        cp.start()
        sent.append(cp)

    def arrived(ref, ssem, rsem):
        copy(ref, ref, ssem, rsem, mate).wait_recv()

    def rows(j, n=CHUNK):
        return pl.ds(j * n, n)

    def blocks_masked(val, mask_ref, i):
        parts = []
        for b in range(COLS // BLOCK):
            keep = jnp.full((BLOCK, BLOCK), mask_ref[i, b], jnp.int32) != 0
            part = val[:, b * BLOCK:(b + 1) * BLOCK].astype(jnp.float32)
            parts.append(jnp.where(keep, part, 0.0))
        return jnp.concatenate(parts, axis=1).astype(jnp.bfloat16)

    n1, k1 = 1 + zl, 1 - zl
    n2, k2 = 3 * zl, zl

    def send_a(n, k, kk, j):
        src = pz.at[n, rows(j)]
        for d in range(2):
            send(src, a1.at[d, k, rows(j)], ys.at[d, kk, j], yr.at[d, k, j], yd[d])

    own_in_a = zh == zl
    inside = zh != zl

    nl = jnp.where(own_in_a, 2 - zl, 3 - 3 * zl)

    def zdev(v):
        return dev(z_=v)

    def z_copies(j):
        src = pz.at[z, rows(j)]
        inner = [
            copy(src, src, zs.at[0, j], zr.at[0, j], zdev(3 - z)),
            copy(src, src, zs.at[1, j], zr.at[0, j], zdev(nl)),
        ]
        outer = copy(src, src, zs.at[0, j], zr.at[1, j], zdev(n1))
        return inner, outer

    def z_start(j):
        inner, outer = z_copies(j)

        @pl.when(own_in_a)
        def _():
            outer.start()

        @pl.when(inside)
        def _():
            for cp in inner:
                cp.start()

    def z_step(j):
        arrived(pz.at[n1, rows(j)], zs.at[0, j], zr.at[0, j])
        @pl.when(inside)
        def _():
            arrived(pz.at[nl, rows(j)], zs.at[0, j], zr.at[1, j])

        src = pz.at[jnp.where(own_in_a, n1, nl), rows(j)]
        send(src, src, zfs.at[j], zfr.at[j], zdev(3 - z))

    def z_far(j):
        @pl.when(inside)
        def _():
            arrived(pz.at[n2, rows(j)], zfs.at[j], zfr.at[j])

    def z_late(j):
        @pl.when(own_in_a)
        def _():
            arrived(pz.at[nl, rows(j)], zfs.at[j], zfr.at[j])

    def z_sent(j):
        inner, outer = z_copies(j)

        @pl.when(own_in_a)
        def _():
            outer.wait_send()

        @pl.when(inside)
        def _():
            for cp in inner:
                cp.wait_send()

    def n2_copies(j):
        src = pz.at[n2, rows(j)]
        return [copy(src, a1.at[d, k2, rows(j)], ys.at[d, 1, j], yr.at[d, k2, j], yd[d]) for d in range(2)]

    def n2_own(j):
        @pl.when(own_in_a)
        def _():
            for cp in n2_copies(j):
                cp.start()

    def n2_far(j):
        @pl.when(inside)
        def _():
            arrived(pz.at[n2, rows(j)], zfs.at[j], zfr.at[j])
            for cp in n2_copies(j):
                cp.start()

        sent.extend(n2_copies(j))

    LAST = 3

    def yb_start():
        for d in range(2):
            send(pz.at[z, rows(LAST)], yb.at[d], ybs.at[d], ybr.at[d], yd[d])

    def yb_step():
        for d in range(2):
            arrived(yb.at[d], ybs.at[d], ybr.at[d])
        for d in range(2):
            part = pl.ds(d * (CHUNK // 2), CHUNK // 2)
            send(yb.at[d, part], yb.at[2, part], yfs.at[d, LAST], yfr.at[d, LAST], yd[d])

    def yb_opp():
        for d in range(2):
            part = pl.ds(d * (CHUNK // 2), CHUNK // 2)
            arrived(yb.at[2, part], yfs.at[d, LAST], yfr.at[d, LAST])

    def yz_copies(i):
        dst = a1.at[i, zl, rows(LAST)]
        near = [
            copy(yb.at[i], dst, yzs.at[0, i], yzr.at[0, i], zdev(3 - z)),
            copy(yb.at[i], dst, yzs.at[1, i], yzr.at[0, i], zdev(nl)),
        ]
        far = copy(yb.at[i], yf.at[i], yzs.at[0, i], yzr.at[1, i], zdev(3 - z))
        return near, far

    def yz_start_outer(i):
        @pl.when(own_in_a)
        def _():
            yz_copies(i)[1].start()
            a1[i, zl, rows(LAST)] = yb[i]

    def yz_start_inner(i):
        @pl.when(inside)
        def _():
            for cp in yz_copies(i)[0]:
                cp.start()

    def yz_pass(i):
        return copy(yf.at[i], a1.at[i, 1 - zl, rows(LAST)], yzs.at[1, i], yzr.at[1, i], zdev(n1))

    def yz_relay(i):
        @pl.when(own_in_a)
        def _():
            arrived(yf.at[i], yzs.at[0, i], yzr.at[1, i])
            yz_pass(i).start()

    def yz_arrived(i):
        arrived(a1.at[i, k1, rows(LAST)], yzs.at[0, i], yzr.at[0, i])

        @pl.when(inside)
        def _():
            arrived(a1.at[i, k2, rows(LAST)], yzs.at[0, i], yzr.at[1, i])

    def yz_sent(i):
        near, far = yz_copies(i)

        @pl.when(own_in_a)
        def _():
            far.wait_send()
            yz_pass(i).wait_send()

        @pl.when(inside)
        def _():
            for cp in near:
                cp.wait_send()

    def p_mask(j):
        load(p_hbm, p_ref, ps, j).wait()
        pz[z, rows(j)] = blocks_masked(p_ref[rows(j)], dm_ref, j)

    p_mask(LAST)
    yb_start()
    p_mask(0)
    z_start(0)

    def s_piece(xx, cc, h):
        return s1.at[xx, pl.ds(pl.multiple_of(cc * ROWS + h * HALF, HALF), HALF)]

    for h in range(2):
        for i in range(2):
            j = 2 * h + i
            load(s_hbm, s_ref, sl, j).wait()
            s1[x, pl.ds(pl.multiple_of(core * ROWS + j * CHUNK, CHUNK), CHUNK)] = blocks_masked(
                s_ref[rows(j)], im_ref, j)
        src = s_piece(x, core, h)
        for d in range(2):
            send(src, src, ss.at[d, h], sr.at[d, h], xs[d])
        send(src, src, sds.at[0, h], sdr.at[0, h], mate)

    def s_part(xx, h, d):
        return s1.at[xx, pl.ds(pl.multiple_of(core * ROWS + h * HALF + d * CHUNK, CHUNK), CHUNK)]

    def s_step(h):
        for d in range(2):
            src = s_piece(xfrom[d], core, h)
            arrived(src, ss.at[d, h], sr.at[d, h])
            part = s_part(xfrom[d], h, d)
            send(part, part, sfs.at[d, h], sfr.at[d, h], xs[d])
            send(src, src, sds.at[1 + d, h], sdr.at[1 + d, h], mate)

    def s_opp(h):
        for d in range(2):
            arrived(s_part(wrap(x + 2), h, d), sfs.at[d, h], sfr.at[d, h])
        src = s_piece(wrap(x + 2), core, h)
        send(src, src, sds.at[3, h], sdr.at[3, h], mate)

    def s_mate(i, h):
        xx = [x, xfrom[0], xfrom[1], wrap(x + 2)][i]
        arrived(s_piece(xx, 1 - core, h), sds.at[i, h], sdr.at[i, h])

    tile = [2 - zh, 3 * zh]

    def b_rows(p, xx, cc, off=0, n=HALF):
        return b2.at[p // 2, xx, pl.ds(pl.multiple_of(cc * ROWS + (p % 2) * HALF + off, n), n)]

    def b_start(p):
        src, dst = pz.at[tile[p // 2], rows(p % 2, HALF)], b_rows(p, x, core)
        for d in range(2):
            send(src, dst, bs.at[p, d], br.at[p, d], xs[d])
        send(src, dst, bds.at[p, 0], bdr.at[p, 0], mate)
        dst[...] = src[...]

    def b_step(p):
        for d in range(2):
            src = b_rows(p, xfrom[d], core)
            arrived(src, bs.at[p, d], br.at[p, d])
            part = b_rows(p, xfrom[d], core, d * CHUNK, CHUNK)
            send(part, part, bfs.at[p, d], bfr.at[p, d], xs[d])
            send(src, src, bds.at[p, 1 + d], bdr.at[p, 1 + d], mate)

    def b_opp(p):
        for d in range(2):
            arrived(b_rows(p, wrap(x + 2), core, d * CHUNK, CHUNK), bfs.at[p, d], bfr.at[p, d])
        src = b_rows(p, wrap(x + 2), core)
        send(src, src, bds.at[p, 3], bdr.at[p, 3], mate)

    xrel = [x, xfrom[0], xfrom[1], wrap(x + 2)]

    def b_mate(p, i):
        arrived(b_rows(p, xrel[i], 1 - core), bds.at[p, i], bdr.at[p, i])

    def a_forward(k, kk, j):
        for d in range(2):
            arrived(a1.at[d, k, rows(j)], ys.at[d, kk, j], yr.at[d, k, j])
        src = a1.at[k, k, rows(j)]
        send(src, a1.at[2, k, rows(j)], yfs.at[k, j], yfr.at[k, j], dev(y_=wrap(y + 1 - 2 * k)))

    def a_opp(j):
        for d in range(2):
            arrived(a1.at[2, d, rows(j)], yfs.at[d, j], yfr.at[d, j])

    def ncols(n):
        return pl.ds(n * NTILE, NTILE)

    def m1_step(left, yy, start, size, first):
        left = jnp.concatenate(left, axis=0)
        for n in range(COLS // NTILE):
            d = jnp.dot(left, s1[yy, :, ncols(n)], preferred_element_type=jnp.float32)
            for k in range(2):
                span, part = pl.ds(start, size), d[k * size:(k + 1) * size]
                if first:
                    acc1[k, span, ncols(n)] = part
                else:
                    acc1[k, span, ncols(n)] += part

    def m1_own(start, size):
        m1_step([pz[2 * zl + k, pl.ds(start, size)] for k in range(2)], y, start, size, True)

    def m1(slot, yy, start, size):
        m1_step([a1[slot, k, pl.ds(start, size)] for k in range(2)], yy, start, size, False)

    yrel = [wrap(y - 1), wrap(y + 1), wrap(y + 2)]

    def rs1_start(j):
        r1s[rows(j)] = acc1[1 - zl, rows(j)].astype(jnp.bfloat16)
        send(r1s.at[rows(j)], r1r.at[rows(j)], r1ss.at[j], r1rs.at[j], zp)

    def f_start(j):
        arrived(r1r.at[rows(j)], r1ss.at[j], r1rs.at[j])
        total = acc1[zl, rows(j)] + r1r[rows(j)].astype(jnp.float32)
        fa[0, rows(j)] = blocks_masked(total, fm_ref, j)
        for d in range(2):
            send(fa.at[0, rows(j)], fa.at[1 + d, rows(j)], fs.at[d, j], fr.at[d, j], yd[d])

    def f_forward(j):
        for d in range(2):
            arrived(fa.at[1 + d, rows(j)], fs.at[d, j], fr.at[d, j])
        d = j % 2
        send(fa.at[1 + d, rows(j)], fa.at[3, rows(j)], ffs.at[j], ffr.at[j], yd[d])

    def f_opp(j):
        arrived(fa.at[3, rows(j)], ffs.at[j], ffr.at[j])

    def diagonal(h):
        at = pl.multiple_of(core * ROWS + h * HALF, HALF)
        square = acc1[zh, rows(h, HALF), pl.ds(at, HALF)]
        r = lax.broadcasted_iota(jnp.int32, (HALF, HALF), 0)
        c = lax.broadcasted_iota(jnp.int32, (HALF, HALF), 1)
        return jnp.sum(jnp.where(r == c, square, 0.0))

    stages = [
        (core, 2, lambda i: dev(c_=lax.rem(core + i, 2))),
        (z, 4, lambda i: dev(z_=lax.rem(z + i, 4))),
        (y, 4, lambda i: dev(y_=lax.rem(y + i, 4))),
        (x, 4, lambda i: dev(x_=lax.rem(x + i, 4))),
    ]

    def e_send(st):
        me, n, target = stages[st]
        for i in range(1, n):
            send(eb.at[st, me], eb.at[st, me], es.at[st, i], er.at[st, i], target(i))

    def e_sum(st):
        me, n, _ = stages[st]
        for i in range(1, n):
            arrived(eb.at[st, lax.rem(me + n - i, n)], es.at[st, i], er.at[st, i])
        total = eb[st, 0]
        for i in range(1, n):
            total = total + eb[st, i]
        return total

    def e_step(st):
        total = e_sum(st)
        eb[st + 1, stages[st + 1][0]] = total
        e_send(st + 1)

    def m2(t, yy, slot, start, size, first):
        span = pl.ds(start, size)

        for n in range(COLS // NTILE):
            d = jnp.dot(fa[slot, span], b2[t, yy, :, ncols(n)], preferred_element_type=jnp.float32)
            if first:
                acc2[t, span, ncols(n)] = d
            else:
                acc2[t, span, ncols(n)] += d

    def m2_half(h, xx, first):
        gap = wrap(xx - y)
        slot = jnp.where(gap == 0, 0, jnp.where(gap == 3, 1, jnp.where(gap == 1, 2, 3)))

        for n in range(COLS // NTILE):
            d = jnp.zeros((ROWS, NTILE), jnp.float32)
            for c in range(2):
                at = pl.ds(c * ROWS + h * HALF, HALF)
                d += jnp.dot(fa[slot, :, at], b2[1, xx, at, ncols(n)], preferred_element_type=jnp.float32)
            if first:
                acc2[1, :, ncols(n)] = d
            else:
                acc2[1, :, ncols(n)] += d

    def rs2_start(j):
        r2s[rows(j)] = acc2[0, rows(j)].astype(jnp.bfloat16)
        send(r2s.at[rows(j)], r2r.at[rows(j)], r2ss.at[j], r2rs.at[j], z2)
        late.append(sent.pop())

    for j in (1, 2):
        p_mask(j)
    two, three = 2 * CHUNK, 3 * CHUNK
    z_start(1)
    n2_own(0)
    yb_step()
    z_step(0)
    send_a(n1, k1, 0, 0)
    z_step(1)
    send_a(n1, k1, 0, 1)
    n2_far(0)
    s_step(0)
    z_start(2)
    n2_own(1)
    z_late(0)
    yb_opp()
    for i in range(3):
        yz_start_outer(i)
    z_start(3)
    n2_far(1)
    s_step(1)
    a_forward(k2, 1, 0)
    a_forward(k1, 0, 0)
    b_start(2)
    z_step(2)
    s_opp(0)
    a_forward(k2, 1, 1)
    z_step(3)
    a_forward(k1, 0, 1)
    for i in range(3):
        yz_start_inner(i)
    z_late(1)
    for i in range(3):
        yz_relay(i)
    s_opp(1)
    b_start(0)
    n2_own(2)
    send_a(n1, k1, 0, 2)
    for i in range(4):
        for h in range(2):
            s_mate(i, h)
    m1_own(0, HALF)
    a_opp(0)
    a_opp(1)
    z_late(2)
    n2_far(2)
    m1(0, yrel[0], 0, HALF)
    m1(1, yrel[1], 0, HALF)
    m1(2, yrel[2], 0, HALF)
    rs1_start(0)
    z_late(3)
    z_far(3)
    rs1_start(1)
    m1_own(three, CHUNK)
    b_start(1)
    a_forward(k1, 0, 2)
    a_forward(k2, 1, 2)
    m1_own(two, CHUNK)
    f_start(0)
    for i in range(3):
        yz_arrived(i)
        m1(i, yrel[i], three, CHUNK)
    a_opp(2)
    rs1_start(3)
    m1(2, yrel[2], two, CHUNK)
    m1(0, yrel[0], two, CHUNK)
    m1(1, yrel[1], two, CHUNK)
    rs1_start(2)
    f_start(1)
    b_step(0)
    b_step(1)
    f_forward(0)
    trace = jnp.where(x == y, diagonal(0) + diagonal(1), 0.0)
    eb[0, core] = jnp.full((8, 128), trace, jnp.float32)
    e_send(0)
    f_forward(1)
    e_step(0)
    b_opp(0)
    f_start(2)
    b_opp(1)
    b_start(3)
    f_opp(0)
    f_start(3)
    for i in range(4):
        b_mate(0, i)
    f_opp(1)
    for i in range(4):
        b_mate(1, i)
    m2(0, y, 0, 0, HALF, True)
    for i in range(2):
        m2(0, yrel[i], 1 + i, 0, HALF, False)
    m2(0, yrel[2], 3, 0, HALF, False)
    rs2_start(0)
    rs2_start(1)
    f_forward(2)
    m2(0, y, 0, two, CHUNK, True)
    for i in range(2):
        m2(0, yrel[i], 1 + i, two, CHUNK, False)
    b_step(2)
    f_forward(3)
    e_step(1)
    f_opp(2)
    m2(0, yrel[2], 3, two, CHUNK, False)
    rs2_start(2)
    b_step(3)
    m2(0, y, 0, three, CHUNK, True)
    for i in range(2):
        m2(0, yrel[i], 1 + i, three, CHUNK, False)
    f_opp(3)
    m2(0, yrel[2], 3, three, CHUNK, False)
    rs2_start(3)
    b_opp(2)
    e_step(2)
    for i in range(4):
        b_mate(2, i)
    for i in range(4):
        m2_half(0, xrel[i], i == 0)
    b_opp(3)
    for i in range(3):
        b_mate(3, i)
        m2_half(1, xrel[i], False)
    b_mate(3, 3)
    m2_half(1, xrel[3], False)
    e_ref[0, 0] = jnp.max(e_sum(3))
    for cp in sent:
        cp.wait_send()
    for i in range(3):
        yz_sent(i)
    for j in range(4):
        z_sent(j)

    def store(j):
        return pltpu.make_async_copy(o_ref.at[rows(j)], o_hbm.at[rows(j)], os.at[j])

    for j in range(4):
        arrived(r2r.at[rows(j)], r2ss.at[j], r2rs.at[j])
        total = acc2[1, rows(j)] + r2r[rows(j)].astype(jnp.float32)
        o_ref[rows(j)] = blocks_masked(total, fm_ref, j)
        store(j).start()
    for cp in late:
        cp.wait_send()
    for j in range(4):
        store(j).wait()


def place(psp_ref, trace_ref, to_ref, to_trace_ref, held, in_sems, out_sems):
    spans = [pl.ds(i * 64, 64) for i in range(8)]
    loads = [pltpu.make_async_copy(psp_ref.at[s], held.at[s], in_sems.at[i]) for i, s in enumerate(spans)]
    stores = [pltpu.make_async_copy(held.at[s], to_ref.at[s], out_sems.at[i]) for i, s in enumerate(spans)]
    for cp in loads:
        cp.start()
    to_trace_ref[0, 0] = trace_ref[0, 0]
    for load, store in zip(loads, stores):
        load.wait()
        store.start()
    for cp in stores:
        cp.wait()


def shards(density, intersection, density_mask, intersection_mask, filter_mask):
    dma = pltpu.SemaphoreType.DMA
    bf16, f32 = jnp.bfloat16, jnp.float32
    hbm, smem = pl.BlockSpec(memory_space=pl.ANY), pl.BlockSpec(memory_space=pltpu.SMEM)
    psp, electrons = pl.pallas_call(
        kernel,
        out_shape=(jax.ShapeDtypeStruct((ROWS, COLS), bf16), jax.ShapeDtypeStruct((1, 1), f32)),
        in_specs=[smem] * 3 + [hbm] * 2,
        out_specs=(hbm, smem),
        scratch_shapes=[
            pltpu.VMEM((ROWS, COLS), bf16),
            pltpu.VMEM((ROWS, COLS), bf16),
            pltpu.VMEM((ROWS, COLS), bf16),
            pltpu.VMEM((4, ROWS, COLS), bf16),
            pltpu.VMEM((3, CHUNK, COLS), bf16),
            pltpu.VMEM((3, CHUNK, COLS), bf16),
            pltpu.VMEM((3, 2, ROWS, COLS), bf16),
            pltpu.VMEM((4, 2 * ROWS, COLS), bf16),
            pltpu.VMEM((2, 4, 2 * ROWS, COLS), bf16),
            pltpu.VMEM((4, ROWS, COLS), bf16),
            pltpu.VMEM((2, ROWS, COLS), f32),
            pltpu.VMEM((2, ROWS, COLS), f32),
            pltpu.VMEM((ROWS, COLS), bf16),
            pltpu.VMEM((ROWS, COLS), bf16),
            pltpu.VMEM((ROWS, COLS), bf16),
            pltpu.VMEM((ROWS, COLS), bf16),
            pltpu.VMEM((4, 4, 8, 128), f32),
            dma((2, 4)), dma((2, 4)), dma((4,)), dma((4,)),
            dma((2, 2, 4)), dma((2, 2, 4)), dma((2, 4)), dma((2, 4)),
            dma((3,)), dma((3,)), dma((2, 3)), dma((2, 3)),
            dma((2, 2)), dma((2, 2)), dma((2, 2)), dma((2, 2)), dma((4, 2)), dma((4, 2)),
            dma((4, 2)), dma((4, 2)), dma((4, 2)), dma((4, 2)), dma((4, 4)), dma((4, 4)),
            dma((4,)), dma((4,)),
            dma((2, 4)), dma((2, 4)), dma((4,)), dma((4,)),
            dma((4,)), dma((4,)),
            dma((4, 4)), dma((4, 4)),
            dma((4,)), dma((4,)), dma((4,)),
        ],
        compiler_params=pltpu.CompilerParams(
            collective_id=0, has_side_effects=True, vmem_limit_bytes=62 * 2**20
        ),
        cost_estimate=pl.CostEstimate(flops=17179869184, bytes_accessed=3 * 2**20, transcendentals=0),
    )(density_mask, intersection_mask, filter_mask, density, intersection)
    psp, electrons = pl.pallas_call(
        place,
        out_shape=(jax.ShapeDtypeStruct((ROWS, COLS), bf16), jax.ShapeDtypeStruct((1, 1), f32)),
        in_specs=[hbm, smem],
        out_specs=(hbm, smem),
        scratch_shapes=[pltpu.VMEM((ROWS, COLS), bf16), dma((8,)), dma((8,))],
    )(psp, electrons)
    return psp, electrons.reshape(())


def solution(mesh):
    placed = (P("row", "col"),) * 5
    return jax.shard_map(
        shards, mesh=mesh, in_specs=placed, out_specs=(P("row", "col"), P()), check_vma=False
    )
```
